256 devices in a mesh: replica: 4 (over x), fsdp: 64 (over z, y, core).
Axes of the slice: x: 4, y: 4, z: 8, core: 2. Of those that a mesh axis runs over, the one named last changes fastest.
Arguments:
- grad_parts: bfloat16 [4, 4096, 12, 1024], P('replica', 'fsdp'), may hold values from -13 to 13
- col_widths: int32 [12], replicated, may hold values from 512 to 1024, as said below
- assignment: int32 [48], replicated, may hold values from 0 to 63, as said below
- left_stat: float32 [128, 1024, 1024], P('fsdp', 'replica'), may hold values from -1 to 40
- right_stat: float32 [128, 1024, 1024], P('fsdp', 'replica'), may hold values from -1 to 40
- left_root: bfloat16 [128, 1024, 1024], P('fsdp', None, 'replica'), may hold values from -0.25 to 5
- right_root: bfloat16 [128, 1024, 1024], P('fsdp', None, 'replica'), may hold values from -0.25 to 5
Outputs:
- update: bfloat16 [4096, 12, 1024], P('fsdp', None, 'replica')
- left_new: float32 [128, 1024, 1024], P('fsdp', 'replica')
- right_new: float32 [128, 1024, 1024], P('fsdp', 'replica')
The draws below stay inside these ranges and needn't reach their ends.
Inputs may be any that keep to these rules, and one draw needn't show every extreme that they name: `assignment`: each worker index is named by at most 2 blocks, and some worker by exactly 2. `col_widths`: exactly one column block is 512 wide, every other one 1024.
All inputs are finite; a program needn't handle non-finite values.
Results may differ from the reference program's by a relative error of at most 0.012.
Values may be sent and summed in bfloat16 or wider, within the bound.
No kernel may reach another device: no remote copies, remote signals or barrier semaphores. Data moves between devices by JAX's collectives and lax.ppermute only.
A program may use at most 128 MiB of HBM per device.

```python
import jax
import jax.numpy as jnp
from jax import lax

D = 4096
BLK = 1024
NCB = 12
NRB = 4
NB = 48
SLOTS = 2
WSLOTS = 128
N_REPLICA = 4
N_FSDP = 64


def diagonal_part(key, lowest, highest, trend):
    position = jnp.arange(BLK, dtype=jnp.float32) / BLK
    spread = jax.random.uniform(key, (WSLOTS, BLK), jnp.float32, jnp.log(lowest), jnp.log(highest))
    return (1.0 + trend * position)[None, :] * jnp.exp(spread)


def assemble(diagonal, offdiag):
    return offdiag + jnp.eye(BLK, dtype=jnp.float32)[None] * diagonal[:, :, None]


def draw_grad_parts(key, part):
    key = jax.random.fold_in(key, 1)
    row_key, col_key, base_key = jax.random.split(key, 3)
    row_pos = (jnp.arange(D) % BLK).astype(jnp.float32) / BLK
    col_pos = jnp.arange(BLK, dtype=jnp.float32) / BLK
    row_scale = jnp.sqrt(1.0 + 2.0 * row_pos) * jnp.exp(jax.random.uniform(row_key, (D,), jnp.float32, -1.15, 1.15))
    col_scale = jnp.sqrt(1.0 + 2.0 * col_pos)[None, :] * jnp.exp(jax.random.uniform(col_key, (NCB, BLK), jnp.float32, -1.15, 1.15))
    base = jnp.clip(jax.random.normal(base_key, (N_REPLICA, D, NCB, BLK), jnp.float32), -5.0, 5.0)
    values = 0.08 * row_scale[None, :, None, None] * col_scale[None, None] * base
    return values.astype(jnp.bfloat16)


def draw_col_widths(key, part):
    key = jax.random.fold_in(key, 2)
    narrow = jax.random.randint(key, (), 0, NCB)
    return jnp.where(jnp.arange(NCB, dtype=jnp.int32) == narrow, BLK // 2, BLK).astype(jnp.int32)


def draw_assignment(key, part):
    key = jax.random.fold_in(key, 3)
    busy_key, block_key, slot_key = jax.random.split(key, 3)
    busiest = jax.random.randint(busy_key, (), 0, N_FSDP)
    shuffled = jax.random.permutation(block_key, NB)
    spare = jax.random.permutation(slot_key, (N_FSDP - 1) * SLOTS)[:NB - SLOTS] // SLOTS
    spare = spare + (spare >= busiest).astype(spare.dtype)
    workers = jnp.concatenate([jnp.full((SLOTS,), busiest, jnp.int32), spare.astype(jnp.int32)])
    return jnp.zeros((NB,), jnp.int32).at[shuffled].set(workers)


def draw_left_stat(key, part):
    key = jax.random.fold_in(key, 4)
    diag_key, off_key = jax.random.split(key)
    diagonal = diagonal_part(diag_key, 1.0, 10.0, 2.0)
    offdiag = 0.1 * jnp.clip(jax.random.normal(off_key, (WSLOTS, BLK, BLK), jnp.float32), -5.0, 5.0)
    return assemble(diagonal, offdiag)


def draw_right_stat(key, part):
    key = jax.random.fold_in(key, 5)
    diag_key, off_key = jax.random.split(key)
    diagonal = diagonal_part(diag_key, 1.0, 10.0, 2.0)
    offdiag = 0.1 * jnp.clip(jax.random.normal(off_key, (WSLOTS, BLK, BLK), jnp.float32), -5.0, 5.0)
    return assemble(diagonal, offdiag)


def draw_left_root(key, part):
    key = jax.random.fold_in(key, 6)
    diag_key, off_key = jax.random.split(key)
    diagonal = diagonal_part(diag_key, 1.0, 2.0, 1.0)
    offdiag = 0.5 / BLK ** 0.5 * jnp.clip(jax.random.normal(off_key, (WSLOTS, BLK, BLK), jnp.float32), -4.0, 4.0)
    return assemble(diagonal, offdiag).astype(jnp.bfloat16)


def draw_right_root(key, part):
    key = jax.random.fold_in(key, 7)
    diag_key, off_key = jax.random.split(key)
    diagonal = diagonal_part(diag_key, 1.0, 2.0, 1.0)
    offdiag = 0.5 / BLK ** 0.5 * jnp.clip(jax.random.normal(off_key, (WSLOTS, BLK, BLK), jnp.float32), -4.0, 4.0)
    return assemble(diagonal, offdiag).astype(jnp.bfloat16)


def setup_inputs(seed: int = 0) -> dict:
    key_of = jax.random.split(jax.random.key(seed), 8)
    return {
        "grad_parts": draw_grad_parts(jax.random.fold_in(key_of[7], 71), 0),
        "col_widths": draw_col_widths(jax.random.fold_in(key_of[7], 71), 0),
        "assignment": draw_assignment(jax.random.fold_in(key_of[7], 71), 0),
        "left_stat": draw_left_stat(jax.random.fold_in(key_of[7], 71), 0),
        "right_stat": draw_right_stat(jax.random.fold_in(key_of[7], 71), 0),
        "left_root": draw_left_root(jax.random.fold_in(key_of[7], 71), 0),
        "right_root": draw_right_root(jax.random.fold_in(key_of[7], 71), 0),
    }


DECAY = 0.99
SHRINKAGE = 0.1
EPSILON = 1e-06

def slot_numbers(assignment):
    blocks = jnp.arange(assignment.shape[0], dtype=jnp.int32)
    same_worker = assignment[:, None] == assignment[None, :]
    earlier = blocks[None, :] < blocks[:, None]
    slot_rank = lax.optimization_barrier(jnp.sum((same_worker & earlier).astype(jnp.int32), axis=1))
    return (assignment * SLOTS + slot_rank).astype(jnp.int32)

def reference(grad_parts, col_widths, assignment, left_stat, right_stat, left_root, right_root):
    col_index = jnp.arange(BLK, dtype=jnp.int32)
    col_mask = (col_index[None, :] < col_widths[:, None]).astype(jnp.float32)
    grad = lax.optimization_barrier(jnp.sum(grad_parts.astype(jnp.float32), axis=0)) * col_mask[None]
    slot_ids = slot_numbers(assignment)
    blocks = jnp.arange(NB, dtype=jnp.int32)

    def one_block(block):
        row_block = (block // NCB).astype(jnp.int32)
        col_block = (block % NCB).astype(jnp.int32)
        slot = slot_ids[block]
        anchor = jnp.zeros((), jnp.int32)
        block_grad = lax.dynamic_slice(grad, (row_block * BLK, col_block, anchor), (BLK, 1, BLK))[:, 0, :]
        width = col_widths[col_block]
        left_gram = jnp.dot(block_grad, block_grad.T, precision=lax.Precision.HIGHEST)
        right_gram = jnp.dot(block_grad.T, block_grad, precision=lax.Precision.HIGHEST)
        left_prod = jnp.dot(left_root[slot], block_grad.astype(jnp.bfloat16), preferred_element_type=jnp.float32).astype(jnp.bfloat16)
        precond = jnp.dot(left_prod, right_root[slot], preferred_element_type=jnp.float32)
        precond = precond * (col_index < width).astype(jnp.float32)[None, :]
        graft = jnp.sqrt(jnp.sum(block_grad * block_grad) / (jnp.sum(precond * precond) + EPSILON))
        return (left_gram, right_gram, (precond * graft).astype(jnp.bfloat16))
    left_grams, right_grams, updates = lax.map(one_block, blocks)
    left_total = (DECAY * left_stat).at[slot_ids].add((1.0 - DECAY) * left_grams)
    right_total = (DECAY * right_stat).at[slot_ids].add((1.0 - DECAY) * right_grams)
    slot_width = jnp.full((WSLOTS,), BLK, jnp.int32).at[slot_ids].set(col_widths[blocks % NCB])
    diag_keep = (col_index[None, :] < slot_width[:, None]).astype(jnp.float32)
    left_trace = jnp.trace(left_total, axis1=1, axis2=2)
    right_trace = lax.optimization_barrier(jnp.sum(jnp.diagonal(right_total, axis1=1, axis2=2) * diag_keep, axis=1))
    unit = jnp.eye(BLK, dtype=jnp.float32)
    left_new = (1.0 - SHRINKAGE) * left_total + SHRINKAGE * (left_trace / BLK)[:, None, None] * unit[None]
    right_scale = SHRINKAGE * right_trace / slot_width.astype(jnp.float32)
    right_new = (1.0 - SHRINKAGE) * right_total + right_scale[:, None, None] * (unit[None] * diag_keep[:, None, :])
    update = updates.reshape(NRB, NCB, BLK, BLK).transpose(0, 2, 1, 3).reshape(D, NCB, BLK)
    return (update, left_new, right_new)
```

```python
import jax
import jax.numpy as jnp
from jax import lax
from jax.sharding import PartitionSpec as P

DECAY = 0.99
SHRINKAGE = 0.1
EPSILON = 1e-06
F32 = jnp.float32
BF16 = jnp.bfloat16


def slot_tables(assignment, workers, slots):
    blocks = jnp.arange(assignment.shape[0], dtype=jnp.int32)
    same_worker = assignment[:, None] == assignment[None, :]
    earlier = blocks[None, :] < blocks[:, None]
    slot_rank = jnp.sum((same_worker & earlier).astype(jnp.int32), axis=1)
    slot_ids = assignment * slots + slot_rank
    wanted = jnp.arange(workers * slots, dtype=jnp.int32)
    slot_hits = (slot_ids[None, :] == wanted[:, None]).astype(jnp.int32)
    filled = jnp.sum(slot_hits, axis=1) > 0
    block_ids = jnp.sum(slot_hits * blocks[None, :], axis=1)
    return (slot_ids, filled, block_ids)


def on_device(grad_parts, col_widths, assignment, left_stat, right_stat, left_root, right_root):
    workers = lax.axis_size("fsdp")
    reps = lax.axis_size("replica")
    me_rep = lax.axis_index("replica")
    me_work = lax.axis_index("fsdp")
    slots, quarter, block_size = left_stat.shape
    rows_dev = grad_parts.shape[1]
    ncols = grad_parts.shape[2]
    per_row = block_size // rows_dev
    groups = workers // per_row
    piece = rows_dev // groups
    nblocks = assignment.shape[0]
    me_group = me_work // per_row

    def turn_x(value, shift):
        pairs = [(a, (a + shift) % reps) for a in range(reps)]
        return lax.ppermute(value, "replica", pairs)

    def turn_group(value, shift):
        pairs = [(a, (a + shift * per_row) % workers) for a in range(workers)]
        return lax.ppermute(value, "fsdp", pairs)

    def sum_x(value):
        total = value
        for shift in range(1, reps):
            total = total + turn_x(value, shift)
        return total

    slot_ids, filled, block_ids = slot_tables(assignment, workers, slots)
    col_index = jnp.arange(block_size, dtype=jnp.int32)
    col_mask = (col_index[None, :] < col_widths[:, None]).astype(F32)

    terms = (grad_parts[0].astype(F32) * col_mask[None]).astype(BF16)

    def columns_of(rep):
        cut = lax.dynamic_slice_in_dim(terms, rep * quarter, quarter, 2)
        return jnp.transpose(cut, (1, 0, 2))

    summed = columns_of(me_rep).astype(F32)
    for shift in (1, 3, 2):
        summed = summed + turn_x(columns_of((me_rep + shift) % reps), shift).astype(F32)
    summed = summed.astype(BF16)

    my_blocks = lax.dynamic_slice_in_dim(block_ids, me_work * slots, slots)
    my_filled = lax.dynamic_slice_in_dim(filled, me_work * slots, slots)
    my_col = my_blocks % ncols
    looked_up = jnp.sum(
        jnp.where(
            my_col[:, None] == jnp.arange(ncols, dtype=jnp.int32)[None, :], col_widths[None, :], 0
        ),
        axis=1,
    )
    my_width = jnp.where(my_filled, looked_up, block_size)
    global_rows = me_rep * quarter + jnp.arange(quarter, dtype=jnp.int32)
    unit_rows = (col_index[None, :] == global_rows[:, None]).astype(F32)
    within_width = (global_rows[None, :] < my_width[:, None]).astype(F32)
    left_diag = jnp.sum(left_stat * unit_rows[None], axis=(1, 2))
    right_diag = jnp.sum(jnp.sum(right_stat * unit_rows[None], axis=2) * within_width, axis=1)
    diag_sums = sum_x(jnp.stack([left_diag, right_diag]))

    left_wide = lax.all_gather(left_root, "replica", axis=0, tiled=False)

    summed = summed.reshape(ncols, groups, piece, quarter)

    def rows_of(group):
        return lax.dynamic_index_in_dim(summed, group, 1, keepdims=False)

    held = [rows_of(me_group)]
    for shift in range(1, groups):
        held.append(turn_group(rows_of((me_group + shift) % groups), shift))
    held = jnp.concatenate(held, axis=0)
    place = ((me_group - block_ids // ncols) % groups) * ncols + block_ids % ncols
    outgoing = jnp.take(held, place, axis=0).reshape(workers, slots, piece, quarter)
    incoming = lax.all_to_all(outgoing, "fsdp", split_axis=0, concat_axis=0, tiled=True)
    g_mine = jnp.transpose(
        incoming.reshape(groups, per_row, slots, piece, quarter), (2, 1, 0, 3, 4)
    ).reshape(slots, block_size, quarter)
    g_mine = jnp.where(my_filled[:, None, None], g_mine, jnp.zeros((), BF16))

    half = block_size // 2
    g_prev = turn_x(g_mine, 1)
    g_next = turn_x(g_mine, reps - 1)
    g_far = jnp.concatenate(
        [turn_x(g_prev[:, :half], 1), turn_x(g_next[:, half:], reps - 1)], axis=1
    )
    g_all = jnp.stack([g_mine, g_prev, g_far, g_next])
    order = (me_rep - jnp.arange(reps, dtype=jnp.int32)) % reps
    g_all = jnp.take(g_all, order, axis=0)

    right_quarters = right_root.reshape(slots, reps, quarter, quarter)
    right_prod = jnp.einsum(
        "xsik,sxkq->siq", g_all, right_quarters, preferred_element_type=F32
    ).astype(BF16)
    right_prod = right_prod.reshape(slots, reps, quarter, quarter)
    precond = jnp.einsum("xsik,sxkq->siq", left_wide, right_prod, preferred_element_type=F32)
    precond = precond * within_width[:, None, :]
    wide = g_all.astype(F32)
    grad_square = jnp.sum(wide * wide, axis=(0, 2, 3))
    precond_square = sum_x(jnp.sum(precond * precond, axis=(1, 2)))
    graft_scale = jnp.sqrt(grad_square / (precond_square + EPSILON))
    graft_update = (precond * graft_scale[:, None, None]).astype(BF16)

    returning = jnp.transpose(
        graft_update.reshape(slots, per_row, groups, piece, quarter), (2, 1, 0, 3, 4)
    ).reshape(workers, slots, piece, quarter)
    arrived = lax.all_to_all(returning, "fsdp", split_axis=0, concat_axis=0, tiled=True)
    arrived = arrived.reshape(workers * slots, piece, quarter)

    own_rows = lax.dynamic_slice_in_dim(g_all, me_rep * quarter, quarter, 2)
    left_gram = jnp.einsum("xsqk,xspk->sqp", own_rows, g_all, preferred_element_type=F32)
    right_gram = jnp.einsum("skq,xskp->sqxp", g_mine, g_all, preferred_element_type=F32)
    right_gram = right_gram.reshape(slots, quarter, block_size)
    left_total = DECAY * left_stat + (1.0 - DECAY) * left_gram
    right_total = DECAY * right_stat + (1.0 - DECAY) * right_gram
    traces = DECAY * diag_sums + (1.0 - DECAY) * grad_square[None, :]
    left_new = (1.0 - SHRINKAGE) * left_total + (SHRINKAGE * traces[0] / block_size)[
        :, None, None
    ] * unit_rows[None]
    right_scale = SHRINKAGE * traces[1] / my_width.astype(F32)
    right_new = (1.0 - SHRINKAGE) * right_total + right_scale[:, None, None] * (
        unit_rows[None] * within_width[:, :, None]
    )

    def blocks_of(group):
        ids = lax.dynamic_slice_in_dim(slot_ids, group * ncols, ncols)
        return jnp.take(arrived, ids, axis=0)

    back = [blocks_of(me_group)]
    for shift in range(1, groups):
        back.append(turn_group(blocks_of((me_group + shift) % groups), shift))
    back = jnp.stack(back)
    order = (me_group - jnp.arange(groups, dtype=jnp.int32)) % groups
    back = jnp.take(back, order, axis=0)
    update = jnp.transpose(back, (0, 2, 1, 3)).reshape(rows_dev, ncols, quarter)
    return (update, left_new, right_new)


def solution(mesh):
    in_specs = (
        P("replica", "fsdp", None, None),
        P(),
        P(),
        P("fsdp", "replica", None),
        P("fsdp", "replica", None),
        P("fsdp", None, "replica"),
        P("fsdp", None, "replica"),
    )
    out_specs = (P("fsdp", None, "replica"), P("fsdp", "replica", None), P("fsdp", "replica", None))
    return jax.shard_map(
        on_device, mesh=mesh, in_specs=in_specs, out_specs=out_specs, check_vma=False
    )
```

```python
import jax
import jax.numpy as jnp
from jax import lax
from jax.experimental import pallas as pl
from jax.experimental.pallas import tpu as pltpu
from jax.sharding import PartitionSpec as P

DECAY = 0.99
SHRINKAGE = 0.1
EPSILON = 1e-06
F32 = jnp.float32
BF16 = jnp.bfloat16
VMEM_LIMIT = 48 * 1024 * 1024
SMEM_SPEC = pl.BlockSpec(memory_space=pltpu.SMEM)


def slot_tables(assignment, workers, slots):
    blocks = jnp.arange(assignment.shape[0], dtype=jnp.int32)
    same_worker = assignment[:, None] == assignment[None, :]
    earlier = blocks[None, :] < blocks[:, None]
    slot_rank = jnp.sum((same_worker & earlier).astype(jnp.int32), axis=1)
    slot_ids = assignment * slots + slot_rank
    wanted = jnp.arange(workers * slots, dtype=jnp.int32)
    slot_hits = (slot_ids[None, :] == wanted[:, None]).astype(jnp.int32)
    filled = jnp.sum(slot_hits, axis=1) > 0
    block_ids = jnp.sum(slot_hits * blocks[None, :], axis=1)
    return (slot_ids, filled, block_ids)


def dot(a, b, contract=(1, 0)):
    dims = (((contract[0],), (contract[1],)), ((), ()))
    return lax.dot_general(a, b, dims, preferred_element_type=F32)


def fold(values):
    rows = values.shape[0]
    part = values[:, :128]
    for first in range(128, values.shape[1], 128):
        part = part + values[:, first : first + 128]
    return jnp.sum(part.reshape(rows // 8, 8, 128), axis=0)


def root_kernel(meta, g0, g1, g3, far0, far1, right, l0, l1, l2, l3, out, sums, far, rights, prods):
    slot = pl.program_id(0)
    me = meta[0]
    width = meta[1 + slot]
    reps = 4
    size = g0.shape[1]
    quarter = g0.shape[2]

    @pl.when(slot == 0)
    def _():
        far[...] = far0[0]

    @pl.when(slot == 1)
    def _():
        far[...] = far1[0]

    def place(turn):
        q = lax.rem(me + reps - turn, reps)
        return pl.ds(pl.multiple_of(q * quarter, quarter), quarter)

    for t in range(reps):
        rights[t * quarter : (t + 1) * quarter, :] = right[0, place(t), :]
    for t in range(reps):
        rows = place(t)
        wide = jnp.concatenate([g0[0, rows, :], g1[0, rows, :], far[rows, :], g3[0, rows, :]], 1)
        prods[t * quarter : (t + 1) * quarter, :] = dot(wide, rights[...]).astype(BF16)
    column = me * quarter + lax.broadcasted_iota(jnp.int32, (quarter, quarter), 1)
    keep = (column < width).astype(F32)
    p_sum = jnp.zeros((8, 128), F32)
    g_sum = jnp.zeros((8, 128), F32)
    for n in range(size // quarter):
        rows = slice(n * quarter, (n + 1) * quarter)
        wide = jnp.concatenate([l0[0, rows, :], l1[0, rows, :], l2[0, rows, :], l3[0, rows, :]], 1)
        value = dot(wide, prods[...]) * keep
        out[0, rows, :] = value
        p_sum = p_sum + fold(value * value)
        own = g0[0, rows, :].astype(F32)
        g_sum = g_sum + fold(own * own)
    sums[0, 0] = p_sum
    sums[0, 1] = g_sum


def scale_kernel(groups, per_row, value, s0, s1, s2, s3, out):
    slots, _, quarter = value.shape
    piece = out.shape[2]
    total = s0[...] + s1[...] + s2[...] + s3[...]
    for s in range(slots):
        p_square = jnp.sum(total[s, 0], keepdims=True)
        g_square = jnp.sum(total[s, 1], keepdims=True)
        scale = jnp.sqrt(g_square / (p_square + EPSILON))
        for p in range(per_row):
            for i in range(groups):
                first = (p * groups + i) * piece
                out[i * per_row + p, s] = (value[s, first : first + piece, :] * scale).astype(BF16)


def stat_kernel(meta, adds, g0, g1, g3, far0, far1, left, right, after, left_new, right_new, far):
    del after
    slot = pl.program_id(0)
    me = meta[0]
    width = meta[1 + slot]
    left_add = adds[0, slot]
    right_add = adds[1, slot]
    reps = 4
    quarter = g0.shape[2]
    keep = 1.0 - SHRINKAGE

    @pl.when(slot == 0)
    def _():
        far[...] = far0[0]

    @pl.when(slot == 1)
    def _():
        far[...] = far1[0]

    def wide(rows):
        return jnp.concatenate([g0[0, rows, :], g1[0, rows, :], far[rows, :], g3[0, rows, :]], 1)

    row = lax.broadcasted_iota(jnp.int32, (quarter, quarter), 0)
    col = lax.broadcasted_iota(jnp.int32, (quarter, quarter), 1)
    first = pl.multiple_of(me * quarter, quarter)
    mine = wide(pl.ds(first, quarter))
    for n in range(reps):
        cols = slice(n * quarter, (n + 1) * quarter)
        gram = dot(mine, wide(cols), (1, 1))
        total = DECAY * left[0, :, cols] + (1.0 - DECAY) * gram
        on = col + n * quarter == row + first
        left_new[0, :, cols] = keep * total + jnp.where(on, left_add, 0.0)
    for t, block in enumerate((g0, g1, None, g3)):
        q = lax.rem(me + reps - t, reps)
        cols = pl.ds(pl.multiple_of(q * quarter, quarter), quarter)
        gram = dot(g0[0], far[...] if block is None else block[0], (0, 0))
        total = keep * (DECAY * right[0, :, cols] + (1.0 - DECAY) * gram)
        if t == 0:
            on = (col == row) & (row + first < width)
            total = total + jnp.where(on, right_add, 0.0)
        right_new[0, :, cols] = total


def on_device(grad_parts, col_widths, assignment, left_stat, right_stat, left_root, right_root):
    workers = lax.axis_size("fsdp")
    reps = lax.axis_size("replica")
    me_rep = lax.axis_index("replica")
    me_work = lax.axis_index("fsdp")
    slots, quarter, block_size = left_stat.shape
    rows_dev = grad_parts.shape[1]
    ncols = grad_parts.shape[2]
    per_row = block_size // rows_dev
    groups = workers // per_row
    piece = rows_dev // groups
    me_group = me_work // per_row

    def turn_x(value, shift):
        pairs = [(a, (a + shift) % reps) for a in range(reps)]
        return lax.ppermute(value, "replica", pairs)

    def turn_group(value, shift):
        pairs = [(a, (a + shift * per_row) % workers) for a in range(workers)]
        return lax.ppermute(value, "fsdp", pairs)

    slot_ids, filled, block_ids = slot_tables(assignment, workers, slots)
    col_index = jnp.arange(block_size, dtype=jnp.int32)
    col_mask = (col_index[None, :] < col_widths[:, None]).astype(F32)
    terms = (grad_parts[0].astype(F32) * col_mask[None]).astype(BF16)

    def columns_of(rep):
        cut = lax.dynamic_slice_in_dim(terms, rep * quarter, quarter, 2)
        return jnp.transpose(cut, (1, 0, 2))

    summed = columns_of(me_rep).astype(F32)
    for shift in (1, 3, 2):
        summed = summed + turn_x(columns_of((me_rep + shift) % reps), shift).astype(F32)
    summed = summed.astype(BF16)
    summed, left_root = lax.optimization_barrier((summed, left_root))

    my_blocks = lax.dynamic_slice_in_dim(block_ids, me_work * slots, slots)
    my_filled = lax.dynamic_slice_in_dim(filled, me_work * slots, slots)
    my_col = my_blocks % ncols
    looked_up = jnp.sum(
        jnp.where(
            my_col[:, None] == jnp.arange(ncols, dtype=jnp.int32)[None, :], col_widths[None, :], 0
        ),
        axis=1,
    )
    my_width = jnp.where(my_filled, looked_up, block_size)
    meta = jnp.concatenate([me_rep[None], my_width]).astype(jnp.int32)
    global_rows = me_rep * quarter + jnp.arange(quarter, dtype=jnp.int32)
    unit_rows = (col_index[None, :] == global_rows[:, None]).astype(F32)
    within_width = (global_rows[None, :] < my_width[:, None]).astype(F32)
    left_diag = jnp.sum(left_stat * unit_rows[None], axis=(1, 2))
    right_diag = jnp.sum(jnp.sum(right_stat * unit_rows[None], axis=2) * within_width, axis=1)
    diag_own = jnp.stack([left_diag, right_diag])

    left_roots = [left_root] + [turn_x(left_root, shift) for shift in (1, 2, 3)]

    summed = summed.reshape(ncols, groups, piece, quarter)

    def rows_of(group):
        return lax.dynamic_index_in_dim(summed, group, 1, keepdims=False)

    held = [rows_of(me_group)]
    for shift in range(1, groups):
        held.append(turn_group(rows_of((me_group + shift) % groups), shift))
    held = jnp.concatenate(held, axis=0)
    place = ((me_group - block_ids // ncols) % groups) * ncols + block_ids % ncols
    outgoing = jnp.take(held, place, axis=0, mode="clip")
    outgoing = outgoing.reshape(workers, slots, piece, quarter)
    incoming = lax.all_to_all(outgoing, "fsdp", split_axis=0, concat_axis=0, tiled=True)
    g_mine = jnp.transpose(
        incoming.reshape(groups, per_row, slots, piece, quarter), (2, 1, 0, 3, 4)
    ).reshape(slots, block_size, quarter)
    g_mine = jnp.where(my_filled[:, None, None], g_mine, jnp.zeros((), BF16))

    g_prev = turn_x(g_mine, 1)
    g_next = turn_x(g_mine, reps - 1)
    g_far0 = turn_x(g_prev[:1], 1)
    g_far1 = turn_x(g_next[1:], reps - 1)
    diag_sums = diag_own
    for shift in (1, 2, 3):
        diag_sums = diag_sums + turn_x(diag_own, shift)

    by_slot = lambda *dims: pl.BlockSpec((1,) + dims, lambda s: (s,) + (0,) * len(dims))
    whole = lambda *dims: pl.BlockSpec(dims, lambda s: (0,) * len(dims))
    col_spec = by_slot(block_size, quarter)
    far_spec = whole(1, block_size, quarter)
    row_spec = by_slot(quarter, block_size)
    col_shape = (slots, block_size, quarter)
    params = pltpu.CompilerParams(vmem_limit_bytes=VMEM_LIMIT)
    precond, sums = pl.pallas_call(
        root_kernel,
        grid=(slots,),
        in_specs=[SMEM_SPEC] + [col_spec] * 3 + [far_spec] * 2 + [col_spec] * 5,
        out_specs=[col_spec, by_slot(2, 8, 128)],
        out_shape=[
            jax.ShapeDtypeStruct(col_shape, F32),
            jax.ShapeDtypeStruct((slots, 2, 8, 128), F32),
        ],
        scratch_shapes=[pltpu.VMEM((block_size, quarter), BF16)] * 3,
        compiler_params=params,
        cost_estimate=pl.CostEstimate(
            flops=8 * block_size * block_size * quarter,
            bytes_accessed=22 * block_size * quarter * 2,
            transcendentals=0,
        ),
        name="root_products",
    )(meta, g_mine, g_prev, g_next, g_far0, g_far1, right_root, *left_roots)
    all_sums = [sums] + [turn_x(sums, shift) for shift in (1, 2, 3)]
    returning = pl.pallas_call(
        lambda *refs: scale_kernel(groups, per_row, *refs),
        out_shape=jax.ShapeDtypeStruct((workers, slots, piece, quarter), BF16),
        compiler_params=params,
        name="graft_scale",
    )(precond, *all_sums)
    arrived = lax.all_to_all(returning, "fsdp", split_axis=0, concat_axis=0, tiled=True)
    arrived = arrived.reshape(workers * slots, piece, quarter)

    grad_square = jnp.sum(sum(s[:, 1] for s in all_sums), axis=(1, 2))
    traces = DECAY * diag_sums + (1.0 - DECAY) * grad_square[None, :]
    divisors = jnp.stack([jnp.full((slots,), block_size, F32), my_width.astype(F32)])
    adds = SHRINKAGE * traces / divisors
    left_new, right_new = pl.pallas_call(
        stat_kernel,
        grid=(slots,),
        in_specs=[SMEM_SPEC] * 2
        + [col_spec] * 3
        + [far_spec] * 2
        + [row_spec] * 2
        + [pl.BlockSpec(memory_space=pl.ANY)],
        out_specs=[row_spec] * 2,
        out_shape=[jax.ShapeDtypeStruct(left_stat.shape, F32)] * 2,
        scratch_shapes=[pltpu.VMEM((block_size, quarter), BF16)],
        compiler_params=params,
        cost_estimate=pl.CostEstimate(
            flops=8 * block_size * block_size * quarter,
            bytes_accessed=40 * block_size * quarter * 2,
            transcendentals=0,
        ),
        name="stat_update",
    )(meta, adds, g_mine, g_prev, g_next, g_far0, g_far1, left_stat, right_stat, returning)

    def blocks_of(group):
        ids = lax.dynamic_slice_in_dim(slot_ids, group * ncols, ncols)
        return jnp.take(arrived, ids, axis=0, mode="clip")

    back = [blocks_of(me_group)]
    for shift in range(1, groups):
        back.append(turn_group(blocks_of((me_group + shift) % groups), shift))
    back = jnp.stack(back)
    order = (me_group - jnp.arange(groups, dtype=jnp.int32)) % groups
    back = jnp.take(back, order, axis=0, mode="clip")
    update = jnp.transpose(back, (0, 2, 1, 3)).reshape(rows_dev, ncols, quarter)
    return (update, left_new, right_new)


def solution(mesh):
    in_specs = (
        P("replica", "fsdp", None, None),
        P(),
        P(),
        P("fsdp", "replica", None),
        P("fsdp", "replica", None),
        P("fsdp", None, "replica"),
        P("fsdp", None, "replica"),
    )
    out_specs = (P("fsdp", None, "replica"), P("fsdp", "replica", None), P("fsdp", "replica", None))
    return jax.shard_map(
        on_device, mesh=mesh, in_specs=in_specs, out_specs=out_specs, check_vma=False
    )
```

```python
import jax
import jax.numpy as jnp
from jax import lax
from jax.experimental import pallas as pl
from jax.experimental.pallas import tpu as pltpu
from jax.sharding import PartitionSpec as P

DECAY = 0.99
SHRINKAGE = 0.1
EPSILON = 1e-06
F32 = jnp.float32
BF16 = jnp.bfloat16
VMEM_LIMIT = 48 * 1024 * 1024
SMEM_SPEC = pl.BlockSpec(memory_space=pltpu.SMEM)


def slot_tables(assignment, workers, slots):
    blocks = jnp.arange(assignment.shape[0], dtype=jnp.int32)
    same_worker = assignment[:, None] == assignment[None, :]
    earlier = blocks[None, :] < blocks[:, None]
    slot_rank = jnp.sum((same_worker & earlier).astype(jnp.int32), axis=1)
    slot_ids = assignment * slots + slot_rank
    wanted = jnp.arange(workers * slots, dtype=jnp.int32)
    slot_hits = (slot_ids[None, :] == wanted[:, None]).astype(jnp.int32)
    filled = jnp.sum(slot_hits, axis=1) > 0
    block_ids = jnp.sum(slot_hits * blocks[None, :], axis=1)
    return (slot_ids, filled, block_ids)


def dot(a, b, contract=(1, 0)):
    dims = (((contract[0],), (contract[1],)), ((), ()))
    return lax.dot_general(a, b, dims, preferred_element_type=F32)


def fold(values):
    rows = values.shape[0]
    part = values[:, :128]
    for first in range(128, values.shape[1], 128):
        part = part + values[:, first : first + 128]
    return jnp.sum(part.reshape(rows // 8, 8, 128), axis=0)


def root_kernel(meta, *refs):
    g0, g1, g3, far0, far1, l0, l1, l3, lfar0, lfar1, right = refs[:11]
    out, sums, far, lfar, rights, prods = refs[11:]
    slot = pl.program_id(0)
    me = meta[0]
    width = meta[1 + slot]
    reps = 4
    size = g0.shape[1]
    quarter = g0.shape[2]

    @pl.when(slot == 0)
    def _():
        far[...] = far0[0]
        lfar[...] = lfar0[0]

    @pl.when(slot == 1)
    def _():
        far[...] = far1[0]
        lfar[...] = lfar1[0]

    def place(turn):
        q = lax.rem(me + reps - turn, reps)
        return pl.ds(pl.multiple_of(q * quarter, quarter), quarter)

    for t in range(reps):
        rights[t * quarter : (t + 1) * quarter, :] = right[0, place(t), :]
    for t in range(reps):
        rows = place(t)
        wide = jnp.concatenate([g0[0, rows, :], g1[0, rows, :], far[rows, :], g3[0, rows, :]], 1)
        prods[t * quarter : (t + 1) * quarter, :] = dot(wide, rights[...]).astype(BF16)
    column = me * quarter + lax.broadcasted_iota(jnp.int32, (quarter, quarter), 1)
    keep = (column < width).astype(F32)
    p_sum = jnp.zeros((8, 128), F32)
    g_sum = jnp.zeros((8, 128), F32)
    for n in range(size // quarter):
        rows = slice(n * quarter, (n + 1) * quarter)
        wide = jnp.concatenate([l0[0, rows, :], l1[0, rows, :], lfar[rows, :], l3[0, rows, :]], 1)
        value = dot(wide, prods[...]) * keep
        out[0, rows, :] = value
        p_sum = p_sum + fold(value * value)
        own = g0[0, rows, :].astype(F32)
        g_sum = g_sum + fold(own * own)
    sums[0, 0] = p_sum
    sums[0, 1] = g_sum


def spread_kernel(place, h0, h1, h2, h3, out, held):
    workers, slots = out.shape[:2]
    for n, ref in enumerate((h0, h1, h2, h3)):
        held[n * ref.shape[0] : (n + 1) * ref.shape[0]] = ref[...]
    for w in range(workers):
        for s in range(slots):
            out[w, s] = held[place[w * slots + s]]


def collect_kernel(wanted, arrived, *outs):
    for n, out in enumerate(outs):
        for j in range(out.shape[0]):
            out[j] = arrived[wanted[n * out.shape[0] + j]]


def scale_kernel(groups, per_row, value, s0, s1, s2, s3, out):
    slots, _, quarter = value.shape
    piece = out.shape[2]
    total = s0[...] + s1[...] + s2[...] + s3[...]
    for s in range(slots):
        p_square = jnp.sum(total[s, 0], keepdims=True)
        g_square = jnp.sum(total[s, 1], keepdims=True)
        scale = jnp.sqrt(g_square / (p_square + EPSILON))
        for p in range(per_row):
            for i in range(groups):
                first = (p * groups + i) * piece
                out[i * per_row + p, s] = (value[s, first : first + piece, :] * scale).astype(BF16)


def stat_kernel(meta, adds, g0, g1, g3, far0, far1, left, right, after, left_new, right_new, far):
    del after
    slot = pl.program_id(0)
    me = meta[0]
    width = meta[1 + slot]
    left_add = adds[0, slot]
    right_add = adds[1, slot]
    reps = 4
    quarter = g0.shape[2]
    keep = 1.0 - SHRINKAGE

    @pl.when(slot == 0)
    def _():
        far[...] = far0[0]

    @pl.when(slot == 1)
    def _():
        far[...] = far1[0]

    def wide(rows):
        return jnp.concatenate([g0[0, rows, :], g1[0, rows, :], far[rows, :], g3[0, rows, :]], 1)

    row = lax.broadcasted_iota(jnp.int32, (quarter, quarter), 0)
    col = lax.broadcasted_iota(jnp.int32, (quarter, quarter), 1)
    first = pl.multiple_of(me * quarter, quarter)
    mine = wide(pl.ds(first, quarter))
    for n in range(reps):
        cols = slice(n * quarter, (n + 1) * quarter)
        gram = dot(mine, wide(cols), (1, 1))
        total = DECAY * left[0, :, cols] + (1.0 - DECAY) * gram
        on = col + n * quarter == row + first
        left_new[0, :, cols] = keep * total + jnp.where(on, left_add, 0.0)
    for t, block in enumerate((g0, g1, None, g3)):
        q = lax.rem(me + reps - t, reps)
        cols = pl.ds(pl.multiple_of(q * quarter, quarter), quarter)
        gram = dot(g0[0], far[...] if block is None else block[0], (0, 0))
        total = keep * (DECAY * right[0, :, cols] + (1.0 - DECAY) * gram)
        if t == 0:
            on = (col == row) & (row + first < width)
            total = total + jnp.where(on, right_add, 0.0)
        right_new[0, :, cols] = total


def on_device(grad_parts, col_widths, assignment, left_stat, right_stat, left_root, right_root):
    workers = lax.axis_size("fsdp")
    reps = lax.axis_size("replica")
    me_rep = lax.axis_index("replica")
    me_work = lax.axis_index("fsdp")
    slots, quarter, block_size = left_stat.shape
    rows_dev = grad_parts.shape[1]
    ncols = grad_parts.shape[2]
    per_row = block_size // rows_dev
    groups = workers // per_row
    piece = rows_dev // groups
    me_group = me_work // per_row

    def turn_x(value, shift):
        pairs = [(a, (a + shift) % reps) for a in range(reps)]
        return lax.ppermute(value, "replica", pairs)

    def turn_group(value, shift):
        pairs = [(a, (a + shift * per_row) % workers) for a in range(workers)]
        return lax.ppermute(value, "fsdp", pairs)

    slot_ids, filled, block_ids = slot_tables(assignment, workers, slots)
    col_index = jnp.arange(block_size, dtype=jnp.int32)
    col_mask = (col_index[None, :] < col_widths[:, None]).astype(F32)
    terms = (grad_parts[0].astype(F32) * col_mask[None]).astype(BF16)

    def columns_of(rep):
        cut = lax.dynamic_slice_in_dim(terms, rep * quarter, quarter, 2)
        return jnp.transpose(cut, (1, 0, 2))

    def add(a, b):
        return (a.astype(F32) + b.astype(F32)).astype(BF16)

    half = ncols // 2
    up, down = columns_of((me_rep + 1) % reps), columns_of((me_rep + 3) % reps)
    far = columns_of((me_rep + 2) % reps)
    relay_up = turn_x(far[:half], 1)
    relay_down = turn_x(far[half:], 3)
    direct_up = turn_x(up[half:], 1)
    direct_down = turn_x(down[:half], 3)
    joint_up = turn_x(add(up[:half], relay_up), 1)
    joint_down = turn_x(add(down[half:], relay_down), 3)
    own = columns_of(me_rep).astype(F32)
    summed = jnp.concatenate(
        [
            own[:half] + joint_up.astype(F32) + direct_down.astype(F32),
            own[half:] + direct_up.astype(F32) + joint_down.astype(F32),
        ]
    ).astype(BF16)
    summed, left_root = lax.optimization_barrier((summed, left_root))

    my_blocks = lax.dynamic_slice_in_dim(block_ids, me_work * slots, slots)
    my_filled = lax.dynamic_slice_in_dim(filled, me_work * slots, slots)
    my_col = my_blocks % ncols
    looked_up = jnp.sum(
        jnp.where(
            my_col[:, None] == jnp.arange(ncols, dtype=jnp.int32)[None, :], col_widths[None, :], 0
        ),
        axis=1,
    )
    my_width = jnp.where(my_filled, looked_up, block_size)
    meta = jnp.concatenate([me_rep[None], my_width]).astype(jnp.int32)
    global_rows = me_rep * quarter + jnp.arange(quarter, dtype=jnp.int32)
    unit_rows = (col_index[None, :] == global_rows[:, None]).astype(F32)
    within_width = (global_rows[None, :] < my_width[:, None]).astype(F32)
    left_diag = jnp.sum(left_stat * unit_rows[None], axis=(1, 2))
    right_diag = jnp.sum(jnp.sum(right_stat * unit_rows[None], axis=2) * within_width, axis=1)
    diag_own = jnp.stack([left_diag, right_diag])

    l_prev = turn_x(left_root, 1)
    l_next = turn_x(left_root, 3)
    l_far0 = turn_x(left_root[:1], 2)
    l_far1 = turn_x(l_next[1:], 3)

    summed = summed.reshape(ncols, groups, piece, quarter)

    def rows_of(group):
        return lax.dynamic_index_in_dim(summed, group, 1, keepdims=False)

    held = [rows_of(me_group)]
    for shift in range(1, groups):
        held.append(turn_group(rows_of((me_group + shift) % groups), shift))
    place = ((me_group - block_ids // ncols) % groups) * ncols + block_ids % ncols
    params = pltpu.CompilerParams(vmem_limit_bytes=VMEM_LIMIT)
    outgoing = pl.pallas_call(
        spread_kernel,
        in_specs=[SMEM_SPEC] + [pl.BlockSpec(memory_space=pltpu.VMEM)] * groups,
        out_shape=jax.ShapeDtypeStruct((workers, slots, piece, quarter), BF16),
        scratch_shapes=[pltpu.VMEM((groups * ncols, piece, quarter), BF16)],
        compiler_params=params,
        name="spread",
    )(place.astype(jnp.int32), *held)
    incoming = lax.all_to_all(outgoing, "fsdp", split_axis=0, concat_axis=0, tiled=True)
    g_mine = jnp.transpose(
        incoming.reshape(groups, per_row, slots, piece, quarter), (2, 1, 0, 3, 4)
    ).reshape(slots, block_size, quarter)
    g_mine = jnp.where(my_filled[:, None, None], g_mine, jnp.zeros((), BF16))

    g_mine, l_prev, l_next, l_far0, l_far1 = lax.optimization_barrier(
        (g_mine, l_prev, l_next, l_far0, l_far1)
    )
    g_prev = turn_x(g_mine, 1)
    g_next = turn_x(g_mine, reps - 1)
    g_far0 = turn_x(g_prev[:1], 1)
    g_far1 = turn_x(g_next[1:], reps - 1)
    diag_sums = diag_own
    for shift in (1, 2, 3):
        diag_sums = diag_sums + turn_x(diag_own, shift)

    by_slot = lambda *dims: pl.BlockSpec((1,) + dims, lambda s: (s,) + (0,) * len(dims))
    whole = lambda *dims: pl.BlockSpec(dims, lambda s: (0,) * len(dims))
    col_spec = by_slot(block_size, quarter)
    far_spec = whole(1, block_size, quarter)
    row_spec = by_slot(quarter, block_size)
    col_shape = (slots, block_size, quarter)
    precond, sums = pl.pallas_call(
        root_kernel,
        grid=(slots,),
        in_specs=[SMEM_SPEC] + ([col_spec] * 3 + [far_spec] * 2) * 2 + [col_spec],
        out_specs=[col_spec, by_slot(2, 8, 128)],
        out_shape=[
            jax.ShapeDtypeStruct(col_shape, F32),
            jax.ShapeDtypeStruct((slots, 2, 8, 128), F32),
        ],
        scratch_shapes=[pltpu.VMEM((block_size, quarter), BF16)] * 4,
        compiler_params=params,
        cost_estimate=pl.CostEstimate(
            flops=8 * block_size * block_size * quarter,
            bytes_accessed=22 * block_size * quarter * 2,
            transcendentals=0,
        ),
        name="root_products",
    )(
        meta,
        *(g_mine, g_prev, g_next, g_far0, g_far1),
        *(left_root, l_prev, l_next, l_far0, l_far1),
        right_root,
    )
    all_sums = [sums] + [turn_x(sums, shift) for shift in (1, 2, 3)]
    returning = pl.pallas_call(
        lambda *refs: scale_kernel(groups, per_row, *refs),
        out_shape=jax.ShapeDtypeStruct((workers, slots, piece, quarter), BF16),
        compiler_params=params,
        name="graft_scale",
    )(precond, *all_sums)
    arrived = lax.all_to_all(returning, "fsdp", split_axis=0, concat_axis=0, tiled=True)
    arrived = arrived.reshape(workers * slots, piece, quarter)

    grad_square = jnp.sum(sum(s[:, 1] for s in all_sums), axis=(1, 2))
    traces = DECAY * diag_sums + (1.0 - DECAY) * grad_square[None, :]
    divisors = jnp.stack([jnp.full((slots,), block_size, F32), my_width.astype(F32)])
    adds = SHRINKAGE * traces / divisors
    left_new, right_new = pl.pallas_call(
        stat_kernel,
        grid=(slots,),
        in_specs=[SMEM_SPEC] * 2
        + [col_spec] * 3
        + [far_spec] * 2
        + [row_spec] * 2
        + [pl.BlockSpec(memory_space=pl.ANY)],
        out_specs=[row_spec] * 2,
        out_shape=[jax.ShapeDtypeStruct(left_stat.shape, F32)] * 2,
        scratch_shapes=[pltpu.VMEM((block_size, quarter), BF16)],
        compiler_params=params,
        cost_estimate=pl.CostEstimate(
            flops=8 * block_size * block_size * quarter,
            bytes_accessed=40 * block_size * quarter * 2,
            transcendentals=0,
        ),
        name="stat_update",
    )(meta, adds, g_mine, g_prev, g_next, g_far0, g_far1, left_stat, right_stat, returning)

    arrived, left_new, right_new = lax.optimization_barrier((arrived, left_new, right_new))
    block = jnp.arange(groups * ncols, dtype=jnp.int32)
    wanted = jnp.take(slot_ids, (block + me_group * ncols) % (groups * ncols), mode="clip")
    back = pl.pallas_call(
        collect_kernel,
        in_specs=[SMEM_SPEC, pl.BlockSpec(memory_space=pltpu.VMEM)],
        out_shape=[jax.ShapeDtypeStruct((ncols, piece, quarter), BF16)] * groups,
        compiler_params=params,
        name="collect",
    )(wanted, arrived)
    back = [back[0]] + [turn_group(back[shift], shift) for shift in range(1, groups)]
    back = jnp.stack(back)
    order = (me_group - jnp.arange(groups, dtype=jnp.int32)) % groups
    back = jnp.take(back, order, axis=0, mode="clip")
    update = jnp.transpose(back, (0, 2, 1, 3)).reshape(rows_dev, ncols, quarter)
    return (update, left_new, right_new)


def solution(mesh):
    in_specs = (
        P("replica", "fsdp", None, None),
        P(),
        P(),
        P("fsdp", "replica", None),
        P("fsdp", "replica", None),
        P("fsdp", None, "replica"),
        P("fsdp", None, "replica"),
    )
    out_specs = (P("fsdp", None, "replica"), P("fsdp", "replica", None), P("fsdp", "replica", None))
    return jax.shard_map(
        on_device, mesh=mesh, in_specs=in_specs, out_specs=out_specs, check_vma=False
    )
```

```python
import jax
import jax.numpy as jnp
from jax import lax
from jax.experimental import pallas as pl
from jax.experimental.pallas import tpu as pltpu
from jax.sharding import PartitionSpec as P

DECAY = 0.99
SHRINKAGE = 0.1
EPSILON = 1e-06
F32 = jnp.float32
BF16 = jnp.bfloat16
VMEM_LIMIT = 20 * 1024 * 1024
RELAY_COST = 10_000_000_000
SMEM_SPEC = pl.BlockSpec(memory_space=pltpu.SMEM)


def slot_tables(assignment, workers, slots):
    blocks = jnp.arange(assignment.shape[0], dtype=jnp.int32)
    same_worker = assignment[:, None] == assignment[None, :]
    earlier = blocks[None, :] < blocks[:, None]
    slot_rank = jnp.sum((same_worker & earlier).astype(jnp.int32), axis=1)
    slot_ids = assignment * slots + slot_rank
    wanted = jnp.arange(workers * slots, dtype=jnp.int32)
    slot_hits = (slot_ids[None, :] == wanted[:, None]).astype(jnp.int32)
    filled = jnp.sum(slot_hits, axis=1) > 0
    block_ids = jnp.sum(slot_hits * blocks[None, :], axis=1)
    return (slot_ids, filled, block_ids)


def dot(a, b, contract=(1, 0)):
    dims = (((contract[0],), (contract[1],)), ((), ()))
    return lax.dot_general(a, b, dims, preferred_element_type=F32)


def fold(values):
    rows = values.shape[0]
    part = values[:, :128]
    for first in range(128, values.shape[1], 128):
        part = part + values[:, first : first + 128]
    return jnp.sum(part.reshape(rows // 8, 8, 128), axis=0)


def relay_kernel(before, behind, up, down):
    count = up.shape[0]
    up[...] = before[:count]
    down[...] = behind[count:]


def product_kernel(meta, arrived, r0, r1, far0, far1, r3, grad, sums, *products):
    slots, groups = grad.shape[:2]
    per_row = arrived.shape[0] // groups
    for s in range(slots):
        filled = meta[1 + slots + s] > 0
        parts = []
        g_sum = jnp.zeros((8, 128), F32)
        for i in range(groups):
            part = arrived[i * per_row : (i + 1) * per_row, s].reshape(grad.shape[2:])
            part = jnp.where(filled, part, jnp.zeros_like(part))
            grad[s, i] = part
            wide = part.astype(F32)
            g_sum = g_sum + fold(wide * wide)
            parts.append(part)
        own = jnp.concatenate(parts, 1)
        rights = (r0.at[2 * s], r1.at[2 * s], (far0, far1)[s].at[0], r3.at[2 * s])
        for product, right in zip(products, rights):
            product[s] = dot(own, right[...]).astype(BF16)
        sums[s] = g_sum


def root_kernel(meta, diags, g_sums, y0, y1, y2, y3, l0, l1, far0, far1, l3, out, sums, prods):
    me = meta[0]
    slots, size, quarter = out.shape
    reps = size // quarter
    piece = quarter // (reps * reps)
    column = me * quarter + lax.broadcasted_iota(jnp.int32, (quarter, quarter), 1)
    for s in range(slots):
        keep = (column < meta[1 + s]).astype(F32)
        for d, rows in enumerate((y0, y1, y2, y3)):
            r = lax.rem(me + d, reps)
            for t in range(reps):
                q = lax.rem(me + reps - t, reps)
                for p in range(reps):
                    source = pl.multiple_of((q * reps + p) * piece, piece)
                    target = pl.multiple_of(((t * reps + p) * reps + r) * piece, piece)
                    prods[pl.ds(target, piece), :] = rows[s, pl.ds(source, piece), :]
        far = (far0, far1)[s]
        n2 = 2 * s + 1
        p_sum = jnp.zeros((8, 128), F32)
        for n in range(reps):
            rows = slice(n * quarter, (n + 1) * quarter)
            lefts = (l0.at[n2, rows], l1.at[n2, rows], far.at[1, rows], l3.at[n2, rows])
            wide = jnp.concatenate([left[...] for left in lefts], 1)
            value = dot(wide, prods[...]) * keep
            out[s, rows] = value
            p_sum = p_sum + fold(value * value)
        sums[s, 0] = p_sum
        sums[s, 1] = g_sums[s]
        sums[s, 2] = jnp.full((8, 128), diags[0, s])
        sums[s, 3] = jnp.full((8, 128), diags[1, s])


def spread_kernel(place, h0, h1, h2, h3, out, held):
    workers, slots = out.shape[:2]
    for n, ref in enumerate((h0, h1, h2, h3)):
        held[n * ref.shape[0] : (n + 1) * ref.shape[0]] = ref[...]
    for w in range(workers):
        for s in range(slots):
            out[w, s] = held[place[w * slots + s]]


def collect_kernel(wanted, arrived, *outs):
    for n, out in enumerate(outs):
        for j in range(out.shape[0]):
            out[j] = arrived[wanted[n * out.shape[0] + j]]


def scale_kernel(groups, per_row, meta, value, s0, s1, s2, s3, out, adds):
    slots, size, _ = value.shape
    piece = out.shape[2]
    total = s0[...] + s1[...] + s2[...] + s3[...]
    for s in range(slots):
        p_square = jnp.sum(total[s, 0], keepdims=True)
        g_square = jnp.sum(total[s, 1], keepdims=True)
        scale = jnp.sqrt(g_square / (p_square + EPSILON))
        for side, width in enumerate((jnp.int32(size), meta[1 + s])):
            trace = DECAY * total[s, 2 + side] + (1.0 - DECAY) * g_square
            adds[side, s] = SHRINKAGE * trace / jnp.full((8, 128), width).astype(F32)
        for p in range(per_row):
            for i in range(groups):
                first = (p * groups + i) * piece
                out[i * per_row + p, s] = (value[s, first : first + piece, :] * scale).astype(BF16)


def stat_kernel(meta, adds, g0, g1, g3, far0, far1, left, right, left_new, right_new, whole):
    me = meta[0]
    slots, quarter, size = left.shape
    reps = size // quarter
    piece = quarter // (reps * reps)
    keep = 1.0 - SHRINKAGE
    row = lax.broadcasted_iota(jnp.int32, (quarter, quarter), 0)
    col = lax.broadcasted_iota(jnp.int32, (quarter, quarter), 1)
    first = pl.multiple_of(me * quarter, quarter)
    for s in range(slots):
        far = (far0, far1)[s]
        for d, block in enumerate((g0.at[s], g3.at[s], far.at[0], g1.at[s])):
            r = lax.rem(me + d, reps)
            for p in range(reps * reps):
                target = pl.multiple_of((p * reps + r) * piece, piece)
                for i in range(reps):
                    whole[pl.ds(target, piece), i * quarter : (i + 1) * quarter] = block[
                        i, p * piece : (p + 1) * piece, :
                    ]
        mine = whole[pl.ds(first, quarter), :]
        for n in range(reps):
            cols = slice(n * quarter, (n + 1) * quarter)
            gram = dot(mine, whole[cols, :], (1, 1))
            total = keep * (DECAY * left[s, :, cols] + (1.0 - DECAY) * gram)
            on = col + n * quarter == row + first
            left_new[s, :, cols] = total + jnp.where(on, adds[0, s, :1, :1], 0.0)
        mine = whole[:, pl.ds(first, quarter)]
        for n in range(reps):
            cols = slice(n * quarter, (n + 1) * quarter)
            gram = dot(mine, whole[:, cols], (0, 0))
            total = keep * (DECAY * right[s, :, cols] + (1.0 - DECAY) * gram)
            on = (col + n * quarter == row + first) & (row + first < meta[1 + s])
            right_new[s, :, cols] = total + jnp.where(on, adds[1, s, :1, :1], 0.0)


def on_device(grad_parts, col_widths, assignment, left_stat, right_stat, left_root, right_root):
    workers = lax.axis_size("fsdp")
    reps = lax.axis_size("replica")
    me_rep = lax.axis_index("replica")
    me_work = lax.axis_index("fsdp")
    slots, quarter, block_size = left_stat.shape
    rows_dev = grad_parts.shape[1]
    ncols = grad_parts.shape[2]
    per_row = block_size // rows_dev
    groups = workers // per_row
    piece = rows_dev // groups
    me_group = me_work // per_row

    def turn_x(value, shift):
        pairs = [(a, (a + shift) % reps) for a in range(reps)]
        return lax.ppermute(value, "replica", pairs)

    def turn_group(value, shift):
        pairs = [(a, (a + shift * per_row) % workers) for a in range(workers)]
        return lax.ppermute(value, "fsdp", pairs)

    slot_ids, filled, block_ids = slot_tables(assignment, workers, slots)
    col_index = jnp.arange(block_size, dtype=jnp.int32)
    col_mask = (col_index[None, :] < col_widths[:, None]).astype(F32)
    terms = (grad_parts[0].astype(F32) * col_mask[None]).astype(BF16)
    terms = jnp.transpose(terms, (1, 0, 2))

    def rows_of(rep):
        return lax.dynamic_slice_in_dim(terms, rep * piece, piece, 1)

    def add(a, b):
        return (a.astype(F32) + b.astype(F32)).astype(BF16)

    half = ncols // 2
    up, down = rows_of((me_rep + 1) % reps), rows_of((me_rep + 3) % reps)
    far = rows_of((me_rep + 2) % reps)
    relay_up = turn_x(far[:half], 1)
    relay_down = turn_x(far[half:], 3)
    direct_up = turn_x(up[half:], 1)
    direct_down = turn_x(down[:half], 3)
    joint_up = turn_x(add(up[:half], relay_up), 1)
    joint_down = turn_x(add(down[half:], relay_down), 3)
    own = rows_of(me_rep).astype(F32)
    summed = jnp.concatenate(
        [
            own[:half] + joint_up.astype(F32) + direct_down.astype(F32),
            own[half:] + direct_up.astype(F32) + joint_down.astype(F32),
        ]
    ).astype(BF16)
    roots = jnp.concatenate([right_root[:1], left_root[:1], right_root[1:], left_root[1:]])
    summed, roots = lax.optimization_barrier((summed, roots))

    my_blocks = lax.dynamic_slice_in_dim(block_ids, me_work * slots, slots)
    my_filled = lax.dynamic_slice_in_dim(filled, me_work * slots, slots)
    my_col = my_blocks % ncols
    looked_up = jnp.sum(
        jnp.where(
            my_col[:, None] == jnp.arange(ncols, dtype=jnp.int32)[None, :], col_widths[None, :], 0
        ),
        axis=1,
    )
    my_width = jnp.where(my_filled, looked_up, block_size)
    meta = jnp.concatenate([me_rep[None], my_width, my_filled]).astype(jnp.int32)
    global_rows = me_rep * quarter + jnp.arange(quarter, dtype=jnp.int32)
    unit_rows = (col_index[None, :] == global_rows[:, None]).astype(F32)
    within_width = (global_rows[None, :] < my_width[:, None]).astype(F32)
    left_diag = jnp.sum(left_stat * unit_rows[None], axis=(1, 2))
    right_diag = jnp.sum(jnp.sum(right_stat * unit_rows[None], axis=2) * within_width, axis=1)
    diag_own = jnp.stack([left_diag, right_diag])

    params = pltpu.CompilerParams(vmem_limit_bytes=VMEM_LIMIT)
    vmem = pl.BlockSpec(memory_space=pltpu.VMEM)

    def relay(before, behind):
        shape = (before.shape[0] // 2,) + before.shape[1:]
        up, down = pl.pallas_call(
            relay_kernel,
            in_specs=[vmem] * 2,
            out_shape=[jax.ShapeDtypeStruct(shape, BF16)] * 2,
            compiler_params=params,
            cost_estimate=pl.CostEstimate(flops=RELAY_COST, bytes_accessed=0, transcendentals=0),
            name="relay",
        )(before, behind)
        return (turn_x(up, 1), turn_x(down, 3))

    roots_prev, roots_next = turn_x(roots, 1), turn_x(roots, 3)
    roots_far = relay(roots_prev, roots_next)

    def columns_of(group):
        return lax.dynamic_slice_in_dim(summed, group * quarter, quarter, 2)

    held = [columns_of(me_group)]
    for shift in range(1, groups):
        held.append(turn_group(columns_of((me_group + shift) % groups), shift))
    place = ((me_group - block_ids // ncols) % groups) * ncols + block_ids % ncols
    outgoing = pl.pallas_call(
        spread_kernel,
        in_specs=[SMEM_SPEC] + [vmem] * groups,
        out_shape=jax.ShapeDtypeStruct((workers, slots, piece, quarter), BF16),
        scratch_shapes=[pltpu.VMEM((groups * ncols, piece, quarter), BF16)],
        compiler_params=params,
        name="spread",
    )(place.astype(jnp.int32), *held)
    incoming = lax.all_to_all(outgoing, "fsdp", split_axis=0, concat_axis=0, tiled=True)

    quarters = jax.ShapeDtypeStruct((slots, quarter, quarter), BF16)
    g_mine, g_sums, *products = pl.pallas_call(
        product_kernel,
        in_specs=[SMEM_SPEC] + [vmem] * 6,
        out_shape=[
            jax.ShapeDtypeStruct((slots, groups, quarter, quarter), BF16),
            jax.ShapeDtypeStruct((slots, 8, 128), F32),
        ]
        + [quarters] * reps,
        compiler_params=params,
        name="right_products",
    )(meta, incoming, roots, roots_prev, *roots_far, roots_next)
    products = [products[0]] + [turn_x(products[n], reps - n) for n in range(1, reps)]
    precond, sums = pl.pallas_call(
        root_kernel,
        in_specs=[SMEM_SPEC] * 2 + [vmem] * 10,
        out_shape=[
            jax.ShapeDtypeStruct((slots, block_size, quarter), F32),
            jax.ShapeDtypeStruct((slots, 4, 8, 128), F32),
        ],
        scratch_shapes=[pltpu.VMEM((block_size, quarter), BF16)],
        compiler_params=params,
        name="left_products",
    )(meta, diag_own, g_sums, *products, roots, roots_prev, *roots_far, roots_next)
    all_sums = [sums] + [turn_x(sums, shift) for shift in (1, 2, 3)]
    all_sums = lax.optimization_barrier((*all_sums, g_mine))
    g_mine = all_sums[reps]
    returning, adds = pl.pallas_call(
        lambda *refs: scale_kernel(groups, per_row, *refs),
        in_specs=[SMEM_SPEC] + [vmem] * 5,
        out_shape=[
            jax.ShapeDtypeStruct((workers, slots, piece, quarter), BF16),
            jax.ShapeDtypeStruct((2, slots, 8, 128), F32),
        ],
        compiler_params=params,
        name="graft_scale",
    )(meta, precond, *all_sums[:reps])
    arrived = lax.all_to_all(returning, "fsdp", split_axis=0, concat_axis=0, tiled=True)
    arrived = arrived.reshape(workers * slots, piece, quarter)

    g_prev = turn_x(g_mine, 1)
    g_next = turn_x(g_mine, reps - 1)
    g_far = relay(g_prev, g_next)
    left_new, right_new = pl.pallas_call(
        stat_kernel,
        in_specs=[SMEM_SPEC] + [vmem] * 8,
        out_shape=[jax.ShapeDtypeStruct(left_stat.shape, F32)] * 2,
        scratch_shapes=[pltpu.VMEM((block_size, block_size), BF16)],
        compiler_params=params,
        cost_estimate=pl.CostEstimate(
            flops=8 * block_size * block_size * quarter,
            bytes_accessed=40 * block_size * quarter * 2,
            transcendentals=0,
        ),
        name="stat_update",
    )(meta, adds, g_mine, g_prev, g_next, *g_far, left_stat, right_stat)
    arrived, left_new, right_new = lax.optimization_barrier((arrived, left_new, right_new))

    block = jnp.arange(groups * ncols, dtype=jnp.int32)
    wanted = jnp.take(slot_ids, (block + me_group * ncols) % (groups * ncols), mode="clip")
    back = pl.pallas_call(
        collect_kernel,
        in_specs=[SMEM_SPEC, pl.BlockSpec(memory_space=pltpu.VMEM)],
        out_shape=[jax.ShapeDtypeStruct((ncols, piece, quarter), BF16)] * groups,
        compiler_params=params,
        name="collect",
    )(wanted, arrived)
    back = [back[0]] + [turn_group(back[shift], shift) for shift in range(1, groups)]
    back = jnp.stack(back)
    order = (me_group - jnp.arange(groups, dtype=jnp.int32)) % groups
    back = jnp.take(back, order, axis=0, mode="clip")
    update = jnp.transpose(back, (0, 2, 1, 3)).reshape(rows_dev, ncols, quarter)
    return (update, left_new, right_new)


def solution(mesh):
    in_specs = (
        P("replica", "fsdp", None, None),
        P(),
        P(),
        P("fsdp", "replica", None),
        P("fsdp", "replica", None),
        P("fsdp", None, "replica"),
        P("fsdp", None, "replica"),
    )
    out_specs = (P("fsdp", None, "replica"), P("fsdp", "replica", None), P("fsdp", "replica", None))
    return jax.shard_map(
        on_device, mesh=mesh, in_specs=in_specs, out_specs=out_specs, check_vma=False
    )
```

```python
import jax
import jax.numpy as jnp
from jax import lax
from jax.experimental import pallas as pl
from jax.experimental.pallas import tpu as pltpu
from jax.sharding import PartitionSpec as P

DECAY = 0.99
SHRINKAGE = 0.1
EPSILON = 1e-06
F32 = jnp.float32
BF16 = jnp.bfloat16
VMEM_LIMIT = 20 * 1024 * 1024
RELAY_COST = 10_000_000_000
COSTS = (10_000_000_000, 10_000_000_000, 5_000_000_000)
SMEM_SPEC = pl.BlockSpec(memory_space=pltpu.SMEM)


def slot_tables(assignment, workers, slots):
    blocks = jnp.arange(assignment.shape[0], dtype=jnp.int32)
    same_worker = assignment[:, None] == assignment[None, :]
    earlier = blocks[None, :] < blocks[:, None]
    slot_rank = jnp.sum((same_worker & earlier).astype(jnp.int32), axis=1)
    slot_ids = assignment * slots + slot_rank
    wanted = jnp.arange(workers * slots, dtype=jnp.int32)
    slot_hits = (slot_ids[None, :] == wanted[:, None]).astype(jnp.int32)
    filled = jnp.sum(slot_hits, axis=1) > 0
    block_ids = jnp.sum(slot_hits * blocks[None, :], axis=1)
    return (slot_ids, filled, block_ids)


def dot(a, b, contract=(1, 0)):
    dims = (((contract[0],), (contract[1],)), ((), ()))
    return lax.dot_general(a, b, dims, preferred_element_type=F32)


def fold(values):
    rows = values.shape[0]
    part = values[:, :128]
    for first in range(128, values.shape[1], 128):
        part = part + values[:, first : first + 128]
    return jnp.sum(part.reshape(rows // 8, 8, 128), axis=0)


def join_kernel(up, relay_up, down, relay_down, joint_up, joint_down):
    joint_up[...] = (up[...].astype(F32) + relay_up[...].astype(F32)).astype(BF16)
    joint_down[...] = (down[...].astype(F32) + relay_down[...].astype(F32)).astype(BF16)


def sum_kernel(group, own, top0, top1, bottom0, bottom1, *outs):
    half = top0.shape[0]
    quarter = outs[0].shape[2]
    for t, out in enumerate(outs):
        g = lax.rem(group[0] + t, len(outs))
        cols = pl.ds(pl.multiple_of(g * quarter, quarter), quarter)
        for rows, a, b in ((slice(0, half), top0, top1), (slice(half, None), bottom0, bottom1)):
            total = own[rows, :, cols].astype(F32) + a[:, :, cols].astype(F32)
            out[rows] = (total + b[:, :, cols].astype(F32)).astype(BF16)


def relay_kernel(before, behind, up, down):
    count = up.shape[0]
    up[...] = before[:count]
    down[...] = behind[count:]


def product_kernel(meta, arrived, r0, r1, r2, r3, grad, sums, *products):
    slots, groups = grad.shape[:2]
    per_row = arrived.shape[0] // groups
    for s in range(slots):
        filled = meta[1 + slots + s] > 0
        parts = []
        g_sum = jnp.zeros((8, 128), F32)
        for i in range(groups):
            part = arrived[i * per_row : (i + 1) * per_row, s].reshape(grad.shape[2:])
            part = jnp.where(filled, part, jnp.zeros_like(part))
            grad[s, i] = part
            wide = part.astype(F32)
            g_sum = g_sum + fold(wide * wide)
            parts.append(part)
        own = jnp.concatenate(parts, 1)
        for product, right in zip(products, (r0, r1, r2, r3)):
            product[s] = dot(own, right[s]).astype(BF16)
        sums[s] = g_sum


def root_kernel(meta, diags, g_sums, y0, y1, y2, y3, l0, l1, l2, l3, out, sums, prods):
    me = meta[0]
    slots, size, quarter = out.shape
    reps = size // quarter
    piece = quarter // (reps * reps)
    column = me * quarter + lax.broadcasted_iota(jnp.int32, (quarter, quarter), 1)
    for s in range(slots):
        keep = (column < meta[1 + s]).astype(F32)
        for d, rows in enumerate((y0, y1, y2, y3)):
            r = lax.rem(me + d, reps)
            for t in range(reps):
                q = lax.rem(me + reps - t, reps)
                for p in range(reps):
                    source = pl.multiple_of((q * reps + p) * piece, piece)
                    target = pl.multiple_of(((t * reps + p) * reps + r) * piece, piece)
                    prods[pl.ds(target, piece), :] = rows[s, pl.ds(source, piece), :]
        p_sum = jnp.zeros((8, 128), F32)
        for n in range(reps):
            rows = slice(n * quarter, (n + 1) * quarter)
            wide = jnp.concatenate([l0[s, rows], l1[s, rows], l2[s, rows], l3[s, rows]], 1)
            value = dot(wide, prods[...]) * keep
            out[s, rows] = value
            p_sum = p_sum + fold(value * value)
        sums[s, 0] = p_sum
        sums[s, 1] = g_sums[s]
        sums[s, 2] = jnp.full((8, 128), diags[0, s])
        sums[s, 3] = jnp.full((8, 128), diags[1, s])


def spread_kernel(place, h0, h1, h2, h3, out, held):
    workers, slots = out.shape[:2]
    for n, ref in enumerate((h0, h1, h2, h3)):
        held[n * ref.shape[0] : (n + 1) * ref.shape[0]] = ref[...]
    for w in range(workers):
        for s in range(slots):
            out[w, s] = held[place[w * slots + s]]


def collect_kernel(wanted, arrived, *outs):
    for n, out in enumerate(outs):
        for j in range(out.shape[0]):
            out[j] = arrived[wanted[n * out.shape[0] + j]]


def scale_kernel(groups, per_row, meta, value, s0, s1, s2, s3, out, adds):
    slots, size, _ = value.shape
    piece = out.shape[2]
    total = s0[...] + s1[...] + s2[...] + s3[...]
    for s in range(slots):
        p_square = jnp.sum(total[s, 0], keepdims=True)
        g_square = jnp.sum(total[s, 1], keepdims=True)
        scale = jnp.sqrt(g_square / (p_square + EPSILON))
        for side, width in enumerate((jnp.int32(size), meta[1 + s])):
            trace = DECAY * total[s, 2 + side] + (1.0 - DECAY) * g_square
            adds[side, s] = SHRINKAGE * trace / jnp.full((8, 128), width).astype(F32)
        for p in range(per_row):
            for i in range(groups):
                first = (p * groups + i) * piece
                out[i * per_row + p, s] = (value[s, first : first + piece, :] * scale).astype(BF16)


def stat_kernel(meta, adds, g0, g1, g3, far0, far1, left, right, left_new, right_new, whole):
    me = meta[0]
    slots, quarter, size = left.shape
    reps = size // quarter
    piece = quarter // (reps * reps)
    keep = 1.0 - SHRINKAGE
    row = lax.broadcasted_iota(jnp.int32, (quarter, quarter), 0)
    col = lax.broadcasted_iota(jnp.int32, (quarter, quarter), 1)
    first = pl.multiple_of(me * quarter, quarter)
    for s in range(slots):
        far = (far0, far1)[s]
        for d, block in enumerate((g0.at[s], g3.at[s], far.at[0], g1.at[s])):
            r = lax.rem(me + d, reps)
            for p in range(reps * reps):
                target = pl.multiple_of((p * reps + r) * piece, piece)
                for i in range(reps):
                    whole[pl.ds(target, piece), i * quarter : (i + 1) * quarter] = block[
                        i, p * piece : (p + 1) * piece, :
                    ]
        mine = whole[pl.ds(first, quarter), :]
        for n in range(reps):
            cols = slice(n * quarter, (n + 1) * quarter)
            gram = dot(mine, whole[cols, :], (1, 1))
            total = keep * (DECAY * left[s, :, cols] + (1.0 - DECAY) * gram)
            on = col + n * quarter == row + first
            left_new[s, :, cols] = total + jnp.where(on, adds[0, s, :1, :1], 0.0)
        mine = whole[:, pl.ds(first, quarter)]
        for n in range(reps):
            cols = slice(n * quarter, (n + 1) * quarter)
            gram = dot(mine, whole[:, cols], (0, 0))
            total = keep * (DECAY * right[s, :, cols] + (1.0 - DECAY) * gram)
            on = (col + n * quarter == row + first) & (row + first < meta[1 + s])
            right_new[s, :, cols] = total + jnp.where(on, adds[1, s, :1, :1], 0.0)


def on_device(grad_parts, col_widths, assignment, left_stat, right_stat, left_root, right_root):
    workers = lax.axis_size("fsdp")
    reps = lax.axis_size("replica")
    me_rep = lax.axis_index("replica")
    me_work = lax.axis_index("fsdp")
    slots, quarter, block_size = left_stat.shape
    rows_dev = grad_parts.shape[1]
    ncols = grad_parts.shape[2]
    per_row = block_size // rows_dev
    groups = workers // per_row
    piece = rows_dev // groups
    me_group = me_work // per_row

    def turn_x(value, shift):
        pairs = [(a, (a + shift) % reps) for a in range(reps)]
        return lax.ppermute(value, "replica", pairs)

    def turn_group(value, shift):
        pairs = [(a, (a + shift * per_row) % workers) for a in range(workers)]
        return lax.ppermute(value, "fsdp", pairs)

    slot_ids, filled, block_ids = slot_tables(assignment, workers, slots)
    col_index = jnp.arange(block_size, dtype=jnp.int32)
    col_mask = (col_index[None, :] < col_widths[:, None]).astype(F32)
    terms = (grad_parts[0].astype(F32) * col_mask[None]).astype(BF16)
    terms = jnp.transpose(terms, (1, 0, 2))

    def rows_of(rep):
        return lax.dynamic_slice_in_dim(terms, rep * piece, piece, 1)

    params = pltpu.CompilerParams(vmem_limit_bytes=VMEM_LIMIT)
    vmem = pl.BlockSpec(memory_space=pltpu.VMEM)
    half = ncols // 2
    up, down = rows_of((me_rep + 1) % reps), rows_of((me_rep + 3) % reps)
    far = rows_of((me_rep + 2) % reps)
    relay_up = turn_x(far[:half], 1)
    relay_down = turn_x(far[half:], 3)
    direct_up = turn_x(up[half:], 1)
    direct_down = turn_x(down[:half], 3)
    joint_up, joint_down = pl.pallas_call(
        join_kernel,
        in_specs=[vmem] * 4,
        out_shape=[jax.ShapeDtypeStruct((half, piece, block_size), BF16)] * 2,
        compiler_params=params,
        cost_estimate=pl.CostEstimate(flops=RELAY_COST, bytes_accessed=0, transcendentals=0),
        name="join",
    )(up[:half], relay_up, down[half:], relay_down)
    joint_up, joint_down = turn_x(joint_up, 1), turn_x(joint_down, 3)
    held = pl.pallas_call(
        sum_kernel,
        in_specs=[SMEM_SPEC] + [vmem] * 5,
        out_shape=[jax.ShapeDtypeStruct((ncols, piece, quarter), BF16)] * groups,
        compiler_params=params,
        name="sum",
    )(me_group[None], rows_of(me_rep), joint_up, direct_down, direct_up, joint_down)
    first, left_root, right_root = lax.optimization_barrier((held[0], left_root, right_root))

    my_blocks = lax.dynamic_slice_in_dim(block_ids, me_work * slots, slots)
    my_filled = lax.dynamic_slice_in_dim(filled, me_work * slots, slots)
    my_col = my_blocks % ncols
    looked_up = jnp.sum(
        jnp.where(
            my_col[:, None] == jnp.arange(ncols, dtype=jnp.int32)[None, :], col_widths[None, :], 0
        ),
        axis=1,
    )
    my_width = jnp.where(my_filled, looked_up, block_size)
    meta = jnp.concatenate([me_rep[None], my_width, my_filled]).astype(jnp.int32)
    local = jnp.arange(quarter, dtype=jnp.int32)
    unit = (local[:, None] == local[None, :]).astype(F32)
    within_width = (me_rep * quarter + local[None, :] < my_width[:, None]).astype(F32)

    def diagonal_of(stat):
        block = lax.dynamic_slice_in_dim(stat, me_rep * quarter, quarter, 2)
        return jnp.sum(block * unit[None], axis=2)

    left_diag = jnp.sum(diagonal_of(left_stat), axis=1)
    right_diag = jnp.sum(diagonal_of(right_stat) * within_width, axis=1)
    diag_own = jnp.stack([left_diag, right_diag])


    def relay(before, behind):
        shape = (before.shape[0] // 2,) + before.shape[1:]
        up, down = pl.pallas_call(
            relay_kernel,
            in_specs=[vmem] * 2,
            out_shape=[jax.ShapeDtypeStruct(shape, BF16)] * 2,
            compiler_params=params,
            cost_estimate=pl.CostEstimate(flops=RELAY_COST, bytes_accessed=0, transcendentals=0),
            name="relay",
        )(before, behind)
        return (turn_x(up, 1), turn_x(down, 3))

    def hold(value, cost):
        anywhere = pl.BlockSpec(memory_space=pl.ANY)
        return pl.pallas_call(
            lambda before, after: None,
            in_specs=[anywhere],
            out_specs=anywhere,
            out_shape=jax.ShapeDtypeStruct(value.shape, value.dtype),
            input_output_aliases={0: 0},
            cost_estimate=pl.CostEstimate(flops=cost, bytes_accessed=0, transcendentals=0),
            name="hold",
        )(value)

    r_prev, r_next = hold(turn_x(right_root, 1), COSTS[2]), hold(turn_x(right_root, 3), COSTS[2])
    r_prev, r_next = lax.optimization_barrier((r_prev, r_next))
    l_prev, l_next = hold(turn_x(left_root, 1), COSTS[0]), hold(turn_x(left_root, 3), COSTS[1])
    r_far, l_far = turn_x(r_prev, 1), turn_x(l_next, 3)

    held = [first] + [turn_group(held[shift], shift) for shift in range(1, groups)]
    place = ((me_group - block_ids // ncols) % groups) * ncols + block_ids % ncols
    outgoing = pl.pallas_call(
        spread_kernel,
        in_specs=[SMEM_SPEC] + [vmem] * groups,
        out_shape=jax.ShapeDtypeStruct((workers, slots, piece, quarter), BF16),
        scratch_shapes=[pltpu.VMEM((groups * ncols, piece, quarter), BF16)],
        compiler_params=params,
        name="spread",
    )(place.astype(jnp.int32), *held)
    incoming = lax.all_to_all(outgoing, "fsdp", split_axis=0, concat_axis=0, tiled=True)

    incoming, l_prev, l_next = lax.optimization_barrier((incoming, l_prev, l_next))
    quarters = jax.ShapeDtypeStruct((slots, quarter, quarter), BF16)
    g_mine, g_sums, *products = pl.pallas_call(
        product_kernel,
        in_specs=[SMEM_SPEC] + [vmem] * 5,
        out_shape=[
            jax.ShapeDtypeStruct((slots, groups, quarter, quarter), BF16),
            jax.ShapeDtypeStruct((slots, 8, 128), F32),
        ]
        + [quarters] * reps,
        compiler_params=params,
        name="right_products",
    )(meta, incoming, right_root, r_prev, r_far, r_next)
    products = [products[0]] + [turn_x(products[n], reps - n) for n in range(1, reps)]
    precond, sums = pl.pallas_call(
        root_kernel,
        in_specs=[SMEM_SPEC] * 2 + [vmem] * 9,
        out_shape=[
            jax.ShapeDtypeStruct((slots, block_size, quarter), F32),
            jax.ShapeDtypeStruct((slots, 4, 8, 128), F32),
        ],
        scratch_shapes=[pltpu.VMEM((block_size, quarter), BF16)],
        compiler_params=params,
        name="left_products",
    )(meta, diag_own, g_sums, *products, left_root, l_prev, l_far, l_next)
    all_sums = [sums] + [turn_x(sums, shift) for shift in (1, 2, 3)]
    *all_sums, g_mine = lax.optimization_barrier((*all_sums, g_mine))
    returning, adds = pl.pallas_call(
        lambda *refs: scale_kernel(groups, per_row, *refs),
        in_specs=[SMEM_SPEC] + [vmem] * 5,
        out_shape=[
            jax.ShapeDtypeStruct((workers, slots, piece, quarter), BF16),
            jax.ShapeDtypeStruct((2, slots, 8, 128), F32),
        ],
        compiler_params=params,
        name="graft_scale",
    )(meta, precond, *all_sums)
    arrived = lax.all_to_all(returning, "fsdp", split_axis=0, concat_axis=0, tiled=True)
    arrived = arrived.reshape(workers * slots, piece, quarter)

    g_prev = turn_x(g_mine, 1)
    g_next = turn_x(g_mine, reps - 1)
    g_far = relay(g_prev, g_next)
    left_new, right_new = pl.pallas_call(
        stat_kernel,
        in_specs=[SMEM_SPEC] + [vmem] * 8,
        out_shape=[jax.ShapeDtypeStruct(left_stat.shape, F32)] * 2,
        scratch_shapes=[pltpu.VMEM((block_size, block_size), BF16)],
        compiler_params=params,
        cost_estimate=pl.CostEstimate(
            flops=8 * block_size * block_size * quarter,
            bytes_accessed=40 * block_size * quarter * 2,
            transcendentals=0,
        ),
        name="stat_update",
    )(meta, adds, g_mine, g_prev, g_next, *g_far, left_stat, right_stat)

    block = jnp.arange(groups * ncols, dtype=jnp.int32)
    wanted = jnp.take(slot_ids, (block + me_group * ncols) % (groups * ncols), mode="clip")
    back = pl.pallas_call(
        collect_kernel,
        in_specs=[SMEM_SPEC, pl.BlockSpec(memory_space=pltpu.VMEM)],
        out_shape=[jax.ShapeDtypeStruct((ncols, piece, quarter), BF16)] * groups,
        compiler_params=params,
        name="collect",
    )(wanted, arrived)
    back = [back[0]] + [turn_group(back[shift], shift) for shift in range(1, groups)]
    back = jnp.stack(back)
    order = (me_group - jnp.arange(groups, dtype=jnp.int32)) % groups
    back = jnp.take(back, order, axis=0, mode="clip")
    update = jnp.transpose(back, (0, 2, 1, 3)).reshape(rows_dev, ncols, quarter)
    return (update, left_new, right_new)


def solution(mesh):
    in_specs = (
        P("replica", "fsdp", None, None),
        P(),
        P(),
        P("fsdp", "replica", None),
        P("fsdp", "replica", None),
        P("fsdp", None, "replica"),
        P("fsdp", None, "replica"),
    )
    out_specs = (P("fsdp", None, "replica"), P("fsdp", "replica", None), P("fsdp", "replica", None))
    return jax.shard_map(
        on_device, mesh=mesh, in_specs=in_specs, out_specs=out_specs, check_vma=False
    )
```

```python
import jax
import jax.numpy as jnp
from jax import lax
from jax.experimental import pallas as pl
from jax.experimental.pallas import tpu as pltpu
from jax.sharding import PartitionSpec as P

DECAY = 0.99
SHRINKAGE = 0.1
EPSILON = 1e-06
F32 = jnp.float32
BF16 = jnp.bfloat16
VMEM_LIMIT = 24 * 1024 * 1024
JOIN_COST = 10_000_000_000
COSTS = (10_000_000_000, 10_000_000_000, 5_000_000_000, 10_000_000_000, 8_000_000_000)
SMEM_SPEC = pl.BlockSpec(memory_space=pltpu.SMEM)


def slot_tables(assignment, workers, slots):
    blocks = jnp.arange(assignment.shape[0], dtype=jnp.int32)
    same_worker = assignment[:, None] == assignment[None, :]
    earlier = blocks[None, :] < blocks[:, None]
    slot_rank = jnp.sum((same_worker & earlier).astype(jnp.int32), axis=1)
    slot_ids = assignment * slots + slot_rank
    wanted = jnp.arange(workers * slots, dtype=jnp.int32)
    slot_hits = (slot_ids[None, :] == wanted[:, None]).astype(jnp.int32)
    filled = jnp.sum(slot_hits, axis=1) > 0
    block_ids = jnp.sum(slot_hits * blocks[None, :], axis=1)
    return (slot_ids, filled, block_ids)


def dot(a, b, contract=(1, 0)):
    dims = (((contract[0],), (contract[1],)), ((), ()))
    return lax.dot_general(a, b, dims, preferred_element_type=F32)


def fold(values):
    rows = values.shape[0]
    part = values[:, :128]
    for first in range(128, values.shape[1], 128):
        part = part + values[:, first : first + 128]
    return jnp.sum(part.reshape(rows // 8, 8, 128), axis=0)


def join_kernel(up, relay_up, down, relay_down, joint_up, joint_down):
    joint_up[...] = (up[...].astype(F32) + relay_up[...].astype(F32)).astype(BF16)
    joint_down[...] = (down[...].astype(F32) + relay_down[...].astype(F32)).astype(BF16)


def sum_kernel(group, own, top0, top1, bottom0, bottom1, *outs):
    half = top0.shape[0]
    quarter = outs[0].shape[2]
    for t, out in enumerate(outs):
        g = lax.rem(group[0] + t, len(outs))
        cols = pl.ds(pl.multiple_of(g * quarter, quarter), quarter)
        for rows, a, b in ((slice(0, half), top0, top1), (slice(half, None), bottom0, bottom1)):
            total = own[rows, :, cols].astype(F32) + a[:, :, cols].astype(F32)
            out[rows] = (total + b[:, :, cols].astype(F32)).astype(BF16)


def split_kernel(whole, first, second):
    first[...] = whole[:1]
    second[...] = whole[1:]


def relay_kernel(before, behind, up, down):
    count = up.shape[0]
    up[...] = before[:count]
    down[...] = behind[count:]


def product_kernel(meta, arrived, r0, r1, r2, r3, grad, sums, *rest):
    products, buffers, done = rest[:4], rest[4], rest[5]
    slots, groups = grad.shape[:2]
    per_row = arrived.shape[0] // groups
    rights = (r0, r1, r3, r2)
    copies = [
        pltpu.make_async_copy(right, buffers.at[n], done.at[n]) for n, right in enumerate(rights)
    ]
    for copy in copies:
        copy.start()
    owns = []
    for s in range(slots):
        filled = meta[1 + slots + s] > 0
        parts = []
        g_sum = jnp.zeros((8, 128), F32)
        for i in range(groups):
            part = arrived[i * per_row : (i + 1) * per_row, s].reshape(grad.shape[2:])
            part = jnp.where(filled, part, jnp.zeros_like(part))
            grad[s, i] = part
            wide = part.astype(F32)
            g_sum = g_sum + fold(wide * wide)
            parts.append(part)
        owns.append(jnp.concatenate(parts, 1))
        sums[s] = g_sum
    for n, product in enumerate((products[0], products[1], products[3], products[2])):
        copies[n].wait()
        for s in range(slots):
            product[s] = dot(owns[s], buffers[n, s]).astype(BF16)


def root_kernel(meta, diags, g_sums, y0, y1, y2, y3, *refs):
    l0, l10, l11, l2, l3, out, sums, prods, buffers, done = refs
    me = meta[0]
    slots, size, quarter = l0.shape
    reps = size // quarter
    piece = out.shape[2]
    per_row = size // (reps * piece)
    copies = []
    for s in range(slots):
        lefts = (l0.at[s], (l10, l11)[s].at[0], l2.at[s], l3.at[s])
        copies.append(
            [
                pltpu.make_async_copy(left, buffers.at[s, t], done.at[s, t])
                for t, left in enumerate(lefts)
            ]
        )
        for copy in copies[s]:
            copy.start()
    column = me * quarter + lax.broadcasted_iota(jnp.int32, (quarter, quarter), 1)
    for s in range(slots):
        keep = (column < meta[1 + s]).astype(F32)
        for d, rows in enumerate((y0, y1, y2, y3)):
            r = lax.rem(me + d, reps)
            for t in range(reps):
                q = lax.rem(me + reps - t, reps)
                for p in range(reps):
                    source = pl.multiple_of((q * reps + p) * piece, piece)
                    target = pl.multiple_of(((t * reps + p) * reps + r) * piece, piece)
                    prods[pl.ds(target, piece), :] = rows[s, pl.ds(source, piece), :]
        for copy in copies[s]:
            copy.wait()
        p_sum = jnp.zeros((8, 128), F32)
        for n in range(reps):
            rows = slice(n * quarter, (n + 1) * quarter)
            wide = jnp.concatenate([buffers[s, t, rows] for t in range(reps)], 1)
            value = dot(wide, prods[...]) * keep
            for p in range(per_row // reps):
                for i in range(reps):
                    first = (p * reps + i) * piece
                    target = i * per_row + n * (per_row // reps) + p
                    out[target, s] = value[first : first + piece].astype(BF16)
            p_sum = p_sum + fold(value * value)
        sums[s, 0] = p_sum
        sums[s, 1] = g_sums[s]
        sums[s, 2] = jnp.full((8, 128), diags[0, s])
        sums[s, 3] = jnp.full((8, 128), diags[1, s])


def spread_kernel(place, h0, h1, h2, h3, out, held):
    workers, slots = out.shape[:2]
    for n, ref in enumerate((h0, h1, h2, h3)):
        held[n * ref.shape[0] : (n + 1) * ref.shape[0]] = ref[...]
    for w in range(workers):
        for s in range(slots):
            out[w, s] = held[place[w * slots + s]]


def collect_kernel(wanted, arrived, table, *outs):
    high = table[...].astype(BF16).astype(F32)
    middle = (table[...] - high).astype(BF16).astype(F32)
    low = table[...] - high - middle
    left = jnp.concatenate([high, middle], 0)
    split = jnp.concatenate([left, jnp.concatenate([low, jnp.zeros_like(low)], 0)], 1)
    for n, out in enumerate(outs):
        count = out.shape[0] - 1
        for j in range(count):
            out[j] = arrived[wanted[n * count + j]]
        out[count] = split.astype(BF16)


def scale_kernel(meta, s0, s1, s2, s3, table, adds):
    slots = adds.shape[1]
    size = 4 * 256
    lane = lax.broadcasted_iota(jnp.int32, table.shape, 1)
    total = s0[...] + s1[...] + s2[...] + s3[...]
    row = jnp.zeros(table.shape, F32)
    for s in range(slots):
        p_square = jnp.sum(total[s, 0], keepdims=True)
        g_square = jnp.sum(total[s, 1], keepdims=True)
        scale = jnp.sqrt(g_square / (p_square + EPSILON))
        row = row + jnp.where(lane == meta[1 + 2 * slots] * slots + s, scale, 0.0)
        for side, width in enumerate((jnp.int32(size), meta[1 + s])):
            trace = DECAY * total[s, 2 + side] + (1.0 - DECAY) * g_square
            adds[side, s] = SHRINKAGE * trace / jnp.full((8, 128), width).astype(F32)
    table[...] = row


def final_kernel(mine, group, b0, b1, b2, b3, out):
    groups, count = out.shape[:2]
    total = jnp.zeros((8, 128), F32)
    for block in (b0, b1, b2, b3):
        split = block[count].astype(F32)
        total = total + split[:8, :128] + split[8:, :128] + split[:8, 128:]
    lane = lax.broadcasted_iota(jnp.int32, (1, 128), 1)
    for j in range(count):
        scale = jnp.sum(jnp.where(lane == mine[j], total[:1], 0.0), axis=1, keepdims=True)
        for t, block in enumerate((b0, b1, b2, b3)):
            g = lax.rem(group[0] + groups - t, groups)
            out[g, j] = (block[j].astype(F32) * scale).astype(BF16)


def stat_kernel(meta, adds, in0, in1, in3, in_far0, in_far1, left_stat, right_stat, *refs):
    left_new, right_new, whole, g0, g1, g3, far0, far1, left, right, done = refs
    me = meta[0]
    slots, quarter, size = left.shape
    sources = (in0, in1, in3, in_far0, in_far1, left_stat, right_stat)
    targets = (g0, g1, g3, far0, far1, left, right)
    copies = [
        pltpu.make_async_copy(source, target, done.at[n])
        for n, (source, target) in enumerate(zip(sources, targets))
    ]
    for copy in copies:
        copy.start()
    for copy in copies[:5]:
        copy.wait()
    reps = size // quarter
    piece = quarter // (reps * reps)
    keep = 1.0 - SHRINKAGE
    row = lax.broadcasted_iota(jnp.int32, (quarter, quarter), 0)
    col = lax.broadcasted_iota(jnp.int32, (quarter, quarter), 1)
    first = pl.multiple_of(me * quarter, quarter)
    for s in range(slots):
        far = (far0, far1)[s]
        for d, block in enumerate((g0.at[s], g3.at[s], far.at[0], g1.at[s])):
            r = lax.rem(me + d, reps)
            for p in range(reps * reps):
                target = pl.multiple_of((p * reps + r) * piece, piece)
                for i in range(reps):
                    whole[pl.ds(target, piece), i * quarter : (i + 1) * quarter] = block[
                        i, p * piece : (p + 1) * piece, :
                    ]
        mine = whole[pl.ds(first, quarter), :]
        if s == 0:
            for copy in copies[5:]:
                copy.wait()
        for n in range(reps):
            cols = slice(n * quarter, (n + 1) * quarter)
            gram = dot(mine, whole[cols, :], (1, 1))
            total = keep * (DECAY * left[s, :, cols] + (1.0 - DECAY) * gram)
            on = col + n * quarter == row + first
            left_new[s, :, cols] = total + jnp.where(on, adds[0, s, :1, :1], 0.0)
        mine = whole[:, pl.ds(first, quarter)]
        for n in range(reps):
            cols = slice(n * quarter, (n + 1) * quarter)
            gram = dot(mine, whole[:, cols], (0, 0))
            total = keep * (DECAY * right[s, :, cols] + (1.0 - DECAY) * gram)
            on = (col + n * quarter == row + first) & (row + first < meta[1 + s])
            right_new[s, :, cols] = total + jnp.where(on, adds[1, s, :1, :1], 0.0)


def on_device(grad_parts, col_widths, assignment, left_stat, right_stat, left_root, right_root):
    workers = lax.axis_size("fsdp")
    reps = lax.axis_size("replica")
    me_rep = lax.axis_index("replica")
    me_work = lax.axis_index("fsdp")
    slots, quarter, block_size = left_stat.shape
    rows_dev = grad_parts.shape[1]
    ncols = grad_parts.shape[2]
    per_row = block_size // rows_dev
    groups = workers // per_row
    piece = rows_dev // groups
    me_group = me_work // per_row

    def turn_x(value, shift):
        pairs = [(a, (a + shift) % reps) for a in range(reps)]
        return lax.ppermute(value, "replica", pairs)

    def turn_group(value, shift):
        pairs = [(a, (a + shift * per_row) % workers) for a in range(workers)]
        return lax.ppermute(value, "fsdp", pairs)

    slot_ids, filled, block_ids = slot_tables(assignment, workers, slots)
    col_index = jnp.arange(block_size, dtype=jnp.int32)
    col_mask = (col_index[None, :] < col_widths[:, None]).astype(F32)
    terms = (grad_parts[0].astype(F32) * col_mask[None]).astype(BF16)
    terms = jnp.transpose(terms, (1, 0, 2))

    def rows_of(rep):
        return lax.dynamic_slice_in_dim(terms, rep * piece, piece, 1)

    params = pltpu.CompilerParams(vmem_limit_bytes=VMEM_LIMIT)
    vmem = pl.BlockSpec(memory_space=pltpu.VMEM)
    half = ncols // 2
    up, down = rows_of((me_rep + 1) % reps), rows_of((me_rep + 3) % reps)
    far = rows_of((me_rep + 2) % reps)
    relay_up = turn_x(far[:half], 1)
    relay_down = turn_x(far[half:], 3)
    direct_up = turn_x(up[half:], 1)
    direct_down = turn_x(down[:half], 3)
    joint_up, joint_down = pl.pallas_call(
        join_kernel,
        in_specs=[vmem] * 4,
        out_shape=[jax.ShapeDtypeStruct((half, piece, block_size), BF16)] * 2,
        compiler_params=params,
        cost_estimate=pl.CostEstimate(flops=JOIN_COST, bytes_accessed=0, transcendentals=0),
        name="join",
    )(up[:half], relay_up, down[half:], relay_down)
    joint_up, joint_down = turn_x(joint_up, 1), turn_x(joint_down, 3)
    joint_up, joint_down, left_root, right_root = lax.optimization_barrier(
        (joint_up, joint_down, left_root, right_root)
    )
    held = pl.pallas_call(
        sum_kernel,
        in_specs=[SMEM_SPEC] + [vmem] * 5,
        out_shape=[jax.ShapeDtypeStruct((ncols, piece, quarter), BF16)] * groups,
        compiler_params=params,
        name="sum",
    )(me_group[None], rows_of(me_rep), joint_up, direct_down, direct_up, joint_down)

    my_blocks = lax.dynamic_slice_in_dim(block_ids, me_work * slots, slots)
    my_filled = lax.dynamic_slice_in_dim(filled, me_work * slots, slots)
    my_col = my_blocks % ncols
    looked_up = jnp.sum(
        jnp.where(
            my_col[:, None] == jnp.arange(ncols, dtype=jnp.int32)[None, :], col_widths[None, :], 0
        ),
        axis=1,
    )
    my_width = jnp.where(my_filled, looked_up, block_size)
    meta = jnp.concatenate([me_rep[None], my_width, my_filled, me_work[None]]).astype(jnp.int32)
    local = jnp.arange(quarter, dtype=jnp.int32)
    unit = (local[:, None] == local[None, :]).astype(F32)
    within_width = (me_rep * quarter + local[None, :] < my_width[:, None]).astype(F32)

    def diagonal_of(stat):
        block = lax.dynamic_slice_in_dim(stat, me_rep * quarter, quarter, 2)
        return jnp.sum(block * unit[None], axis=2)

    left_diag = jnp.sum(diagonal_of(left_stat), axis=1)
    right_diag = jnp.sum(diagonal_of(right_stat) * within_width, axis=1)
    diag_own = jnp.stack([left_diag, right_diag])


    def relay(before, behind):
        shape = (before.shape[0] // 2,) + before.shape[1:]
        up, down = pl.pallas_call(
            relay_kernel,
            in_specs=[vmem] * 2,
            out_shape=[jax.ShapeDtypeStruct(shape, BF16)] * 2,
            compiler_params=params,
            cost_estimate=pl.CostEstimate(flops=COSTS[3], bytes_accessed=0, transcendentals=0),
            name="relay",
        )(before, behind)
        return (turn_x(up, 1), turn_x(down, 3))

    anywhere = pl.BlockSpec(memory_space=pl.ANY)

    def hold(value, cost):
        return pl.pallas_call(
            lambda before, after: None,
            in_specs=[anywhere],
            out_specs=anywhere,
            out_shape=jax.ShapeDtypeStruct(value.shape, value.dtype),
            input_output_aliases={0: 0},
            cost_estimate=pl.CostEstimate(flops=cost, bytes_accessed=0, transcendentals=0),
            name="hold",
        )(value)

    r_prev, r_next = hold(turn_x(right_root, 1), COSTS[2]), hold(turn_x(right_root, 3), COSTS[2])
    r_prev, r_next = lax.optimization_barrier((r_prev, r_next))
    left0, left1 = pl.pallas_call(
        split_kernel,
        in_specs=[vmem],
        out_shape=[jax.ShapeDtypeStruct((1, block_size, quarter), BF16)] * slots,
        compiler_params=params,
        name="split",
    )(left_root)
    l_prev0, l_next = hold(turn_x(left0, 1), COSTS[0]), hold(turn_x(left_root, 3), COSTS[1])
    l_prev0, left1 = lax.optimization_barrier((l_prev0, left1))
    l_prev1 = turn_x(left1, 1)
    r_far, l_far = turn_x(r_prev, 1), turn_x(l_next, 3)

    held = [held[0]] + [turn_group(held[shift], shift) for shift in range(1, groups)]
    place = ((me_group - block_ids // ncols) % groups) * ncols + block_ids % ncols
    outgoing = pl.pallas_call(
        spread_kernel,
        in_specs=[SMEM_SPEC] + [vmem] * groups,
        out_shape=jax.ShapeDtypeStruct((workers, slots, piece, quarter), BF16),
        scratch_shapes=[pltpu.VMEM((groups * ncols, piece, quarter), BF16)],
        compiler_params=params,
        name="spread",
    )(place.astype(jnp.int32), *held)
    incoming = lax.all_to_all(outgoing, "fsdp", split_axis=0, concat_axis=0, tiled=True)

    incoming, l_prev0, l_next = lax.optimization_barrier((incoming, l_prev0, l_next))
    quarters = jax.ShapeDtypeStruct((slots, quarter, quarter), BF16)
    g_mine, g_sums, *products = pl.pallas_call(
        product_kernel,
        in_specs=[SMEM_SPEC, vmem] + [anywhere] * 4,
        scratch_shapes=[
            pltpu.VMEM((reps, slots, block_size, quarter), BF16),
            pltpu.SemaphoreType.DMA((reps,)),
        ],
        out_shape=[
            jax.ShapeDtypeStruct((slots, groups, quarter, quarter), BF16),
            jax.ShapeDtypeStruct((slots, 8, 128), F32),
        ]
        + [quarters] * reps,
        compiler_params=params,
        name="right_products",
    )(meta, incoming, right_root, r_prev, r_far, r_next)
    products = [products[0]] + [turn_x(products[n], reps - n) for n in range(1, reps)]
    returning, sums = pl.pallas_call(
        root_kernel,
        in_specs=[SMEM_SPEC] * 2 + [vmem] * 5 + [anywhere] * 5,
        out_shape=[
            jax.ShapeDtypeStruct((workers, slots, piece, quarter), BF16),
            jax.ShapeDtypeStruct((slots, 4, 8, 128), F32),
        ],
        scratch_shapes=[
            pltpu.VMEM((block_size, quarter), BF16),
            pltpu.VMEM((slots, reps, block_size, quarter), BF16),
            pltpu.SemaphoreType.DMA((slots, reps)),
        ],
        compiler_params=params,
        name="left_products",
    )(meta, diag_own, g_sums, *products, left_root, l_prev0, l_prev1, l_far, l_next)
    returning, sums, g_mine = lax.optimization_barrier((returning, sums, g_mine))
    arrived = lax.all_to_all(returning, "fsdp", split_axis=0, concat_axis=0, tiled=True)
    arrived = arrived.reshape(workers * slots, piece, quarter)
    all_sums = [sums] + [turn_x(sums, shift) for shift in (1, 2, 3)]
    table, adds = pl.pallas_call(
        scale_kernel,
        in_specs=[SMEM_SPEC] + [vmem] * 4,
        out_shape=[
            jax.ShapeDtypeStruct((8, workers * slots), F32),
            jax.ShapeDtypeStruct((2, slots, 8, 128), F32),
        ],
        compiler_params=params,
        cost_estimate=pl.CostEstimate(flops=COSTS[4], bytes_accessed=0, transcendentals=0),
        name="graft_scale",
    )(meta, *all_sums)
    g_prev = turn_x(g_mine, 1)
    g_next = turn_x(g_mine, reps - 1)
    g_prev, g_next, table = lax.optimization_barrier((g_prev, g_next, table))
    distance = 1
    while distance < per_row:
        pairs = [(a, a ^ distance) for a in range(workers)]
        table = table + lax.ppermute(table, "fsdp", pairs)
        distance *= 2

    g_far = relay(g_prev, g_next)
    left_new, right_new = pl.pallas_call(
        stat_kernel,
        in_specs=[SMEM_SPEC, vmem] + [anywhere] * 7,
        out_shape=[jax.ShapeDtypeStruct(left_stat.shape, F32)] * 2,
        scratch_shapes=[
            pltpu.VMEM((block_size, block_size), BF16),
            *[pltpu.VMEM(g_mine.shape, BF16)] * 3,
            *[pltpu.VMEM(g_far[0].shape, BF16)] * 2,
            pltpu.VMEM(left_stat.shape, F32),
            pltpu.VMEM(right_stat.shape, F32),
            pltpu.SemaphoreType.DMA((7,)),
        ],
        compiler_params=pltpu.CompilerParams(vmem_limit_bytes=56 * 1024 * 1024),
        cost_estimate=pl.CostEstimate(
            flops=8 * block_size * block_size * quarter,
            bytes_accessed=40 * block_size * quarter * 2,
            transcendentals=0,
        ),
        name="stat_update",
    )(meta, adds, g_mine, g_prev, g_next, *g_far, left_stat, right_stat)

    block = jnp.arange(groups * ncols, dtype=jnp.int32)
    wanted = jnp.take(slot_ids, (block + me_group * ncols) % (groups * ncols), mode="clip")
    back = pl.pallas_call(
        collect_kernel,
        in_specs=[SMEM_SPEC, vmem, vmem],
        out_shape=[jax.ShapeDtypeStruct((ncols + 1, piece, quarter), BF16)] * groups,
        compiler_params=params,
        name="collect",
    )(wanted, arrived, table)
    back = [back[0]] + [turn_group(back[shift], shift) for shift in range(1, groups)]
    update = pl.pallas_call(
        final_kernel,
        in_specs=[SMEM_SPEC] * 2 + [vmem] * groups,
        out_shape=jax.ShapeDtypeStruct((groups, ncols, piece, quarter), BF16),
        compiler_params=params,
        name="final",
    )(wanted[:ncols], me_group[None], *back)
    update = jnp.transpose(update, (0, 2, 1, 3)).reshape(rows_dev, ncols, quarter)
    return (update, left_new, right_new)


def solution(mesh):
    in_specs = (
        P("replica", "fsdp", None, None),
        P(),
        P(),
        P("fsdp", "replica", None),
        P("fsdp", "replica", None),
        P("fsdp", None, "replica"),
        P("fsdp", None, "replica"),
    )
    out_specs = (P("fsdp", None, "replica"), P("fsdp", "replica", None), P("fsdp", "replica", None))
    return jax.shard_map(
        on_device, mesh=mesh, in_specs=in_specs, out_specs=out_specs, check_vma=False
    )
```

```python
import jax
import jax.numpy as jnp
from jax import lax
from jax.experimental import pallas as pl
from jax.experimental.pallas import tpu as pltpu
from jax.sharding import PartitionSpec as P

DECAY = 0.99
SHRINKAGE = 0.1
EPSILON = 1e-06
F32 = jnp.float32
BF16 = jnp.bfloat16
VMEM_LIMIT = 24 * 1024 * 1024
JOIN_COST = 10_000_000_000
COSTS = (10_000_000_000, 10_000_000_000, 5_000_000_000, 4_000_000_000, 0)
SMEM_SPEC = pl.BlockSpec(memory_space=pltpu.SMEM)


def slot_tables(assignment, workers, slots):
    blocks = jnp.arange(assignment.shape[0], dtype=jnp.int32)
    same_worker = assignment[:, None] == assignment[None, :]
    earlier = blocks[None, :] < blocks[:, None]
    slot_rank = jnp.sum((same_worker & earlier).astype(jnp.int32), axis=1)
    slot_ids = assignment * slots + slot_rank
    wanted = jnp.arange(workers * slots, dtype=jnp.int32)
    slot_hits = (slot_ids[None, :] == wanted[:, None]).astype(jnp.int32)
    filled = jnp.sum(slot_hits, axis=1) > 0
    block_ids = jnp.sum(slot_hits * blocks[None, :], axis=1)
    return (slot_ids, filled, block_ids)


def dot(a, b, contract=(1, 0)):
    dims = (((contract[0],), (contract[1],)), ((), ()))
    return lax.dot_general(a, b, dims, preferred_element_type=F32)


def fold(values):
    rows = values.shape[0]
    part = values[:, :128]
    for first in range(128, values.shape[1], 128):
        part = part + values[:, first : first + 128]
    return jnp.sum(part.reshape(rows // 8, 8, 128), axis=0)


def join_kernel(up, relay_up, down, relay_down, joint_up, joint_down):
    joint_up[...] = (up[...].astype(F32) + relay_up[...].astype(F32)).astype(BF16)
    joint_down[...] = (down[...].astype(F32) + relay_down[...].astype(F32)).astype(BF16)


def sum_kernel(group, own, top0, top1, bottom0, bottom1, *outs):
    half = top0.shape[0]
    quarter = outs[0].shape[2]
    for t, out in enumerate(outs):
        g = lax.rem(group[0] + t, len(outs))
        cols = pl.ds(pl.multiple_of(g * quarter, quarter), quarter)
        for rows, a, b in ((slice(0, half), top0, top1), (slice(half, None), bottom0, bottom1)):
            total = own[rows, :, cols].astype(F32) + a[:, :, cols].astype(F32)
            out[rows] = (total + b[:, :, cols].astype(F32)).astype(BF16)


def split_kernel(whole, first, second):
    first[...] = whole[:1]
    second[...] = whole[1:]


def product_kernel(meta, arrived, r0, r1, r2, r3, grad, sums, *rest):
    products, buffers, done = rest[:4], rest[4], rest[5]
    slots, groups = grad.shape[:2]
    per_row = arrived.shape[0] // groups
    rights = (r0, r1, r3, r2)
    copies = [
        pltpu.make_async_copy(right, buffers.at[n], done.at[n]) for n, right in enumerate(rights)
    ]
    for copy in copies:
        copy.start()
    owns = []
    for s in range(slots):
        filled = meta[1 + slots + s] > 0
        parts = []
        g_sum = jnp.zeros((8, 128), F32)
        for i in range(groups):
            part = arrived[i * per_row : (i + 1) * per_row, s].reshape(grad.shape[2:])
            part = jnp.where(filled, part, jnp.zeros_like(part))
            grad[s, i] = part
            wide = part.astype(F32)
            g_sum = g_sum + fold(wide * wide)
            parts.append(part)
        owns.append(jnp.concatenate(parts, 1))
        sums[s] = g_sum
    for n, product in enumerate((products[0], products[1], products[3], products[2])):
        copies[n].wait()
        for s in range(slots):
            product[s] = dot(owns[s], buffers[n, s]).astype(BF16)


def root_kernel(meta, diags, g_sums, y0, y1, y2, y3, *refs):
    l0, l10, l11, l2, l3, out, sums, prods, buffers, done = refs
    me = meta[0]
    slots, size, quarter = l0.shape
    reps = size // quarter
    piece = out.shape[2]
    per_row = size // (reps * piece)
    copies = []
    for s in range(slots):
        lefts = (l0.at[s], (l10, l11)[s].at[0], l2.at[s], l3.at[s])
        copies.append(
            [
                pltpu.make_async_copy(left, buffers.at[s, t], done.at[s, t])
                for t, left in enumerate(lefts)
            ]
        )
        for copy in copies[s]:
            copy.start()
    column = me * quarter + lax.broadcasted_iota(jnp.int32, (quarter, quarter), 1)
    for s in range(slots):
        keep = (column < meta[1 + s]).astype(F32)
        for d, rows in enumerate((y0, y1, y2, y3)):
            r = lax.rem(me + d, reps)
            for t in range(reps):
                q = lax.rem(me + reps - t, reps)
                for p in range(reps):
                    source = pl.multiple_of((q * reps + p) * piece, piece)
                    target = pl.multiple_of(((t * reps + p) * reps + r) * piece, piece)
                    prods[pl.ds(target, piece), :] = rows[s, pl.ds(source, piece), :]
        for copy in copies[s]:
            copy.wait()
        p_sum = jnp.zeros((8, 128), F32)
        for n in range(reps):
            rows = slice(n * quarter, (n + 1) * quarter)
            wide = jnp.concatenate([buffers[s, t, rows] for t in range(reps)], 1)
            value = dot(wide, prods[...]) * keep
            for p in range(per_row // reps):
                for i in range(reps):
                    first = (p * reps + i) * piece
                    target = i * per_row + n * (per_row // reps) + p
                    out[target, s] = value[first : first + piece].astype(BF16)
            p_sum = p_sum + fold(value * value)
        sums[s, 0] = p_sum
        sums[s, 1] = g_sums[s]
        sums[s, 2] = jnp.full((8, 128), diags[0, s])
        sums[s, 3] = jnp.full((8, 128), diags[1, s])


def spread_kernel(place, h0, h1, h2, h3, out, held):
    workers, slots = out.shape[:2]
    for n, ref in enumerate((h0, h1, h2, h3)):
        held[n * ref.shape[0] : (n + 1) * ref.shape[0]] = ref[...]
    for w in range(workers):
        for s in range(slots):
            out[w, s] = held[place[w * slots + s]]


def collect_kernel(wanted, arrived, table, *outs):
    high = table[...].astype(BF16).astype(F32)
    middle = (table[...] - high).astype(BF16).astype(F32)
    low = table[...] - high - middle
    left = jnp.concatenate([high, middle], 0)
    split = jnp.concatenate([left, jnp.concatenate([low, jnp.zeros_like(low)], 0)], 1)
    for n, out in enumerate(outs):
        count = out.shape[0] - 1
        for j in range(count):
            out[j] = arrived[wanted[n * count + j]]
        out[count] = split.astype(BF16)


def scale_kernel(meta, s0, s1, s2, s3, table, adds):
    slots = adds.shape[1]
    size = 4 * 256
    lane = lax.broadcasted_iota(jnp.int32, table.shape, 1)
    total = s0[...] + s1[...] + s2[...] + s3[...]
    row = jnp.zeros(table.shape, F32)
    for s in range(slots):
        p_square = jnp.sum(total[s, 0], keepdims=True)
        g_square = jnp.sum(total[s, 1], keepdims=True)
        scale = jnp.sqrt(g_square / (p_square + EPSILON))
        row = row + jnp.where(lane == meta[1 + 2 * slots] * slots + s, scale, 0.0)
        for side, width in enumerate((jnp.int32(size), meta[1 + s])):
            trace = DECAY * total[s, 2 + side] + (1.0 - DECAY) * g_square
            adds[side, s] = SHRINKAGE * trace / jnp.full((8, 128), width).astype(F32)
    table[...] = row


def final_kernel(mine, group, b0, b1, b2, b3, out):
    groups, count = out.shape[:2]
    total = jnp.zeros((8, 128), F32)
    for block in (b0, b1, b2, b3):
        split = block[count].astype(F32)
        total = total + split[:8, :128] + split[8:, :128] + split[:8, 128:]
    lane = lax.broadcasted_iota(jnp.int32, (1, 128), 1)
    for j in range(count):
        scale = jnp.sum(jnp.where(lane == mine[j], total[:1], 0.0), axis=1, keepdims=True)
        for t, block in enumerate((b0, b1, b2, b3)):
            g = lax.rem(group[0] + groups - t, groups)
            out[g, j] = (block[j].astype(F32) * scale).astype(BF16)


def stat_kernel(meta, adds, in0, in1, in3, in_far, left_stat, right_stat, *refs):
    left_new, right_new, whole, g0, g1, g3, far, left, right, left_out, right_out, done = refs
    me = meta[0]
    slots, quarter, size = left.shape
    reps = size // quarter
    piece = quarter // (reps * reps)
    loads = []
    for s in range(slots):
        sources = (in0.at[s], in1.at[s], in3.at[s], in_far.at[s])
        targets = (g0.at[s], g1.at[s], g3.at[s], far.at[s])
        sources += (left_stat.at[s], right_stat.at[s])
        targets += (left.at[s], right.at[s])
        loads.append(
            [
                pltpu.make_async_copy(source, target, done.at[s, n])
                for n, (source, target) in enumerate(zip(sources, targets))
            ]
        )
    for copies in loads:
        for copy in copies:
            copy.start()
    keep = 1.0 - SHRINKAGE
    row = lax.broadcasted_iota(jnp.int32, (quarter, quarter), 0)
    col = lax.broadcasted_iota(jnp.int32, (quarter, quarter), 1)
    first = pl.multiple_of(me * quarter, quarter)
    stores = []
    for s in range(slots):
        for copy in loads[s][:4]:
            copy.wait()
        for d, block in enumerate((g0.at[s], g3.at[s], far.at[s], g1.at[s])):
            r = lax.rem(me + d, reps)
            for p in range(reps * reps):
                target = pl.multiple_of((p * reps + r) * piece, piece)
                for i in range(reps):
                    whole[pl.ds(target, piece), i * quarter : (i + 1) * quarter] = block[
                        i, p * piece : (p + 1) * piece, :
                    ]
        for copy in loads[s][4:]:
            copy.wait()
        mine = whole[pl.ds(first, quarter), :]
        for n in range(reps):
            cols = slice(n * quarter, (n + 1) * quarter)
            gram = dot(mine, whole[cols, :], (1, 1))
            total = keep * DECAY * left[s, :, cols] + keep * (1.0 - DECAY) * gram
            on = col + n * quarter == row + first
            left_out[s, :, cols] = total + jnp.where(on, adds[0, s, :1, :1], 0.0)
        stores.append(pltpu.make_async_copy(left_out.at[s], left_new.at[s], done.at[s, 6]))
        stores[-1].start()
        mine = whole[:, pl.ds(first, quarter)].T
        for n in range(reps):
            cols = slice(n * quarter, (n + 1) * quarter)
            gram = dot(mine, whole[:, cols])
            total = keep * DECAY * right[s, :, cols] + keep * (1.0 - DECAY) * gram
            on = (col + n * quarter == row + first) & (row + first < meta[1 + s])
            right_out[s, :, cols] = total + jnp.where(on, adds[1, s, :1, :1], 0.0)
        stores.append(pltpu.make_async_copy(right_out.at[s], right_new.at[s], done.at[s, 7]))
        stores[-1].start()
    for copy in stores:
        copy.wait()


def on_device(grad_parts, col_widths, assignment, left_stat, right_stat, left_root, right_root):
    workers = lax.axis_size("fsdp")
    reps = lax.axis_size("replica")
    me_rep = lax.axis_index("replica")
    me_work = lax.axis_index("fsdp")
    slots, quarter, block_size = left_stat.shape
    rows_dev = grad_parts.shape[1]
    ncols = grad_parts.shape[2]
    per_row = block_size // rows_dev
    groups = workers // per_row
    piece = rows_dev // groups
    me_group = me_work // per_row

    def turn_x(value, shift):
        pairs = [(a, (a + shift) % reps) for a in range(reps)]
        return lax.ppermute(value, "replica", pairs)

    def turn_group(value, shift):
        pairs = [(a, (a + shift * per_row) % workers) for a in range(workers)]
        return lax.ppermute(value, "fsdp", pairs)

    slot_ids, filled, block_ids = slot_tables(assignment, workers, slots)
    col_index = jnp.arange(block_size, dtype=jnp.int32)
    col_mask = (col_index[None, :] < col_widths[:, None]).astype(F32)
    terms = (grad_parts[0].astype(F32) * col_mask[None]).astype(BF16)
    terms = jnp.transpose(terms, (1, 0, 2))

    def rows_of(rep):
        return lax.dynamic_slice_in_dim(terms, rep * piece, piece, 1)

    params = pltpu.CompilerParams(vmem_limit_bytes=VMEM_LIMIT)
    vmem = pl.BlockSpec(memory_space=pltpu.VMEM)
    half = ncols // 2
    up, down = rows_of((me_rep + 1) % reps), rows_of((me_rep + 3) % reps)
    far = rows_of((me_rep + 2) % reps)
    relay_up = turn_x(far[:half], 1)
    relay_down = turn_x(far[half:], 3)
    direct_up = turn_x(up[half:], 1)
    direct_down = turn_x(down[:half], 3)
    joint_up, joint_down = pl.pallas_call(
        join_kernel,
        in_specs=[vmem] * 4,
        out_shape=[jax.ShapeDtypeStruct((half, piece, block_size), BF16)] * 2,
        compiler_params=params,
        cost_estimate=pl.CostEstimate(flops=JOIN_COST, bytes_accessed=0, transcendentals=0),
        name="join",
    )(up[:half], relay_up, down[half:], relay_down)
    joint_up, joint_down = turn_x(joint_up, 1), turn_x(joint_down, 3)
    joint_up, joint_down, left_root, right_root = lax.optimization_barrier(
        (joint_up, joint_down, left_root, right_root)
    )
    held = pl.pallas_call(
        sum_kernel,
        in_specs=[SMEM_SPEC] + [vmem] * 5,
        out_shape=[jax.ShapeDtypeStruct((ncols, piece, quarter), BF16)] * groups,
        compiler_params=params,
        name="sum",
    )(me_group[None], rows_of(me_rep), joint_up, direct_down, direct_up, joint_down)

    my_blocks = lax.dynamic_slice_in_dim(block_ids, me_work * slots, slots)
    my_filled = lax.dynamic_slice_in_dim(filled, me_work * slots, slots)
    my_col = my_blocks % ncols
    looked_up = jnp.sum(
        jnp.where(
            my_col[:, None] == jnp.arange(ncols, dtype=jnp.int32)[None, :], col_widths[None, :], 0
        ),
        axis=1,
    )
    my_width = jnp.where(my_filled, looked_up, block_size)
    meta = jnp.concatenate([me_rep[None], my_width, my_filled, me_work[None]]).astype(jnp.int32)
    local = jnp.arange(quarter, dtype=jnp.int32)
    unit = (local[:, None] == local[None, :]).astype(F32)
    within_width = (me_rep * quarter + local[None, :] < my_width[:, None]).astype(F32)

    def diagonal_of(stat):
        block = lax.dynamic_slice_in_dim(stat, me_rep * quarter, quarter, 2)
        return jnp.sum(block * unit[None], axis=2)

    left_diag = jnp.sum(diagonal_of(left_stat), axis=1)
    right_diag = jnp.sum(diagonal_of(right_stat) * within_width, axis=1)
    diag_own = jnp.stack([left_diag, right_diag])


    anywhere = pl.BlockSpec(memory_space=pl.ANY)

    def hold(value, cost):
        return pl.pallas_call(
            lambda before, after: None,
            in_specs=[anywhere],
            out_specs=anywhere,
            out_shape=jax.ShapeDtypeStruct(value.shape, value.dtype),
            input_output_aliases={0: 0},
            cost_estimate=pl.CostEstimate(flops=cost, bytes_accessed=0, transcendentals=0),
            name="hold",
        )(value)

    r_prev, r_next = hold(turn_x(right_root, 1), COSTS[2]), hold(turn_x(right_root, 3), COSTS[2])
    r_prev, r_next = lax.optimization_barrier((r_prev, r_next))
    left0, left1 = pl.pallas_call(
        split_kernel,
        in_specs=[vmem],
        out_shape=[jax.ShapeDtypeStruct((1, block_size, quarter), BF16)] * slots,
        compiler_params=params,
        name="split",
    )(left_root)
    l_prev0, l_next = hold(turn_x(left0, 1), COSTS[0]), hold(turn_x(left_root, 3), COSTS[1])
    l_prev0, left1 = lax.optimization_barrier((l_prev0, left1))
    l_prev1 = turn_x(left1, 1)
    r_far, l_far = turn_x(r_prev, 1), turn_x(l_next, 3)

    held = [held[0]] + [turn_group(held[shift], shift) for shift in range(1, groups)]
    place = ((me_group - block_ids // ncols) % groups) * ncols + block_ids % ncols
    outgoing = pl.pallas_call(
        spread_kernel,
        in_specs=[SMEM_SPEC] + [vmem] * groups,
        out_shape=jax.ShapeDtypeStruct((workers, slots, piece, quarter), BF16),
        scratch_shapes=[pltpu.VMEM((groups * ncols, piece, quarter), BF16)],
        compiler_params=params,
        name="spread",
    )(place.astype(jnp.int32), *held)
    incoming = lax.all_to_all(outgoing, "fsdp", split_axis=0, concat_axis=0, tiled=True)

    incoming, l_prev0, l_next = lax.optimization_barrier((incoming, l_prev0, l_next))
    quarters = jax.ShapeDtypeStruct((slots, quarter, quarter), BF16)
    g_mine, g_sums, *products = pl.pallas_call(
        product_kernel,
        in_specs=[SMEM_SPEC, vmem] + [anywhere] * 4,
        scratch_shapes=[
            pltpu.VMEM((reps, slots, block_size, quarter), BF16),
            pltpu.SemaphoreType.DMA((reps,)),
        ],
        out_shape=[
            jax.ShapeDtypeStruct((slots, groups, quarter, quarter), BF16),
            jax.ShapeDtypeStruct((slots, 8, 128), F32),
        ]
        + [quarters] * reps,
        compiler_params=params,
        name="right_products",
    )(meta, incoming, right_root, r_prev, r_far, r_next)
    products = [products[0]] + [turn_x(products[n], reps - n) for n in range(1, reps)]
    returning, sums = pl.pallas_call(
        root_kernel,
        in_specs=[SMEM_SPEC] * 2 + [vmem] * 5 + [anywhere] * 5,
        out_shape=[
            jax.ShapeDtypeStruct((workers, slots, piece, quarter), BF16),
            jax.ShapeDtypeStruct((slots, 4, 8, 128), F32),
        ],
        scratch_shapes=[
            pltpu.VMEM((block_size, quarter), BF16),
            pltpu.VMEM((slots, reps, block_size, quarter), BF16),
            pltpu.SemaphoreType.DMA((slots, reps)),
        ],
        compiler_params=params,
        name="left_products",
    )(meta, diag_own, g_sums, *products, left_root, l_prev0, l_prev1, l_far, l_next)
    returning, sums, g_mine = lax.optimization_barrier((returning, sums, g_mine))
    arrived = lax.all_to_all(returning, "fsdp", split_axis=0, concat_axis=0, tiled=True)
    arrived = arrived.reshape(workers * slots, piece, quarter)
    all_sums = [sums] + [turn_x(sums, shift) for shift in (1, 2, 3)]
    table, adds = pl.pallas_call(
        scale_kernel,
        in_specs=[SMEM_SPEC] + [vmem] * 4,
        out_shape=[
            jax.ShapeDtypeStruct((8, workers * slots), F32),
            jax.ShapeDtypeStruct((2, slots, 8, 128), F32),
        ],
        compiler_params=params,
        cost_estimate=pl.CostEstimate(flops=COSTS[4], bytes_accessed=0, transcendentals=0),
        name="graft_scale",
    )(meta, *all_sums)
    g_prev = turn_x(g_mine, 1)
    g_next = turn_x(g_mine, reps - 1)
    g_prev, g_next = hold(g_prev, COSTS[3]), hold(g_next, COSTS[3])
    g_prev, g_next, table = lax.optimization_barrier((g_prev, g_next, table))
    distance = 1
    while distance < per_row:
        pairs = [(a, a ^ distance) for a in range(workers)]
        table = table + lax.ppermute(table, "fsdp", pairs)
        distance *= 2

    g_far = turn_x(g_prev, 1)
    left_new, right_new = pl.pallas_call(
        stat_kernel,
        in_specs=[SMEM_SPEC, vmem] + [anywhere] * 6,
        out_specs=[anywhere] * 2,
        out_shape=[jax.ShapeDtypeStruct(left_stat.shape, F32)] * 2,
        scratch_shapes=[
            pltpu.VMEM((block_size, block_size), BF16),
            *[pltpu.VMEM(g_mine.shape, BF16)] * 4,
            *[pltpu.VMEM(left_stat.shape, F32)] * 4,
            pltpu.SemaphoreType.DMA((slots, 8)),
        ],
        compiler_params=pltpu.CompilerParams(vmem_limit_bytes=56 * 1024 * 1024),
        cost_estimate=pl.CostEstimate(
            flops=8 * block_size * block_size * quarter,
            bytes_accessed=40 * block_size * quarter * 2,
            transcendentals=0,
        ),
        name="stat_update",
    )(meta, adds, g_mine, g_prev, g_next, g_far, left_stat, right_stat)

    block = jnp.arange(groups * ncols, dtype=jnp.int32)
    wanted = jnp.take(slot_ids, (block + me_group * ncols) % (groups * ncols), mode="clip")
    back = pl.pallas_call(
        collect_kernel,
        in_specs=[SMEM_SPEC, vmem, vmem],
        out_shape=[jax.ShapeDtypeStruct((ncols + 1, piece, quarter), BF16)] * groups,
        compiler_params=params,
        name="collect",
    )(wanted, arrived, table)
    back = [back[0]] + [turn_group(back[shift], shift) for shift in range(1, groups)]
    update = pl.pallas_call(
        final_kernel,
        in_specs=[SMEM_SPEC] * 2 + [vmem] * groups,
        out_shape=jax.ShapeDtypeStruct((groups, ncols, piece, quarter), BF16),
        compiler_params=params,
        name="final",
    )(wanted[:ncols], me_group[None], *back)
    update = jnp.transpose(update, (0, 2, 1, 3)).reshape(rows_dev, ncols, quarter)
    return (update, left_new, right_new)


def solution(mesh):
    in_specs = (
        P("replica", "fsdp", None, None),
        P(),
        P(),
        P("fsdp", "replica", None),
        P("fsdp", "replica", None),
        P("fsdp", None, "replica"),
        P("fsdp", None, "replica"),
    )
    out_specs = (P("fsdp", None, "replica"), P("fsdp", "replica", None), P("fsdp", "replica", None))
    return jax.shard_map(
        on_device, mesh=mesh, in_specs=in_specs, out_specs=out_specs, check_vma=False
    )
```

```python
import jax
import jax.numpy as jnp
from jax import lax
from jax.experimental import pallas as pl
from jax.experimental.pallas import tpu as pltpu
from jax.sharding import PartitionSpec as P

DECAY = 0.99
SHRINKAGE = 0.1
EPSILON = 1e-06
F32 = jnp.float32
BF16 = jnp.bfloat16
VMEM_LIMIT = 24 * 1024 * 1024
JOIN_COST = 10_000_000_000
COSTS = (10_000_000_000, 10_000_000_000, 5_000_000_000, 4_000_000_000, 8_000_000_000)
SMEM_SPEC = pl.BlockSpec(memory_space=pltpu.SMEM)


def slot_tables(assignment, workers, slots):
    blocks = jnp.arange(assignment.shape[0], dtype=jnp.int32)
    same_worker = assignment[:, None] == assignment[None, :]
    earlier = blocks[None, :] < blocks[:, None]
    slot_rank = jnp.sum((same_worker & earlier).astype(jnp.int32), axis=1)
    slot_ids = assignment * slots + slot_rank
    wanted = jnp.arange(workers * slots, dtype=jnp.int32)
    slot_hits = (slot_ids[None, :] == wanted[:, None]).astype(jnp.int32)
    filled = jnp.sum(slot_hits, axis=1) > 0
    block_ids = jnp.sum(slot_hits * blocks[None, :], axis=1)
    return (slot_ids, filled, block_ids)


def dot(a, b, contract=(1, 0)):
    dims = (((contract[0],), (contract[1],)), ((), ()))
    return lax.dot_general(a, b, dims, preferred_element_type=F32)


def fold(values):
    rows = values.shape[0]
    part = values[:, :128]
    for first in range(128, values.shape[1], 128):
        part = part + values[:, first : first + 128]
    return jnp.sum(part.reshape(rows // 8, 8, 128), axis=0)


def join_kernel(up, relay_up, down, relay_down, joint_up, joint_down):
    joint_up[...] = (up[...].astype(F32) + relay_up[...].astype(F32)).astype(BF16)
    joint_down[...] = (down[...].astype(F32) + relay_down[...].astype(F32)).astype(BF16)


def sum_kernel(group, own, top0, top1, bottom0, bottom1, *outs):
    half = top0.shape[0]
    quarter = outs[0].shape[2]
    for t, out in enumerate(outs):
        g = lax.rem(group[0] + t, len(outs))
        cols = pl.ds(pl.multiple_of(g * quarter, quarter), quarter)
        for rows, a, b in ((slice(0, half), top0, top1), (slice(half, None), bottom0, bottom1)):
            total = own[rows, :, cols].astype(F32) + a[:, :, cols].astype(F32)
            out[rows] = (total + b[:, :, cols].astype(F32)).astype(BF16)


def split_kernel(whole, first, second):
    first[...] = whole[:1]
    second[...] = whole[1:]


def product_kernel(meta, arrived, r0, r1, r2, r3, grad, sums, *rest):
    products, buffers, done = rest[:4], rest[4], rest[5]
    slots, groups = grad.shape[:2]
    per_row = arrived.shape[0] // groups
    rights = (r0, r1, r3, r2)
    copies = [
        pltpu.make_async_copy(right, buffers.at[n], done.at[n]) for n, right in enumerate(rights)
    ]
    for copy in copies:
        copy.start()
    owns = []
    for s in range(slots):
        filled = meta[1 + slots + s] > 0
        parts = []
        g_sum = jnp.zeros((8, 128), F32)
        for i in range(groups):
            part = arrived[i * per_row : (i + 1) * per_row, s].reshape(grad.shape[2:])
            part = jnp.where(filled, part, jnp.zeros_like(part))
            grad[s, i] = part
            wide = part.astype(F32)
            g_sum = g_sum + fold(wide * wide)
            parts.append(part)
        owns.append(jnp.concatenate(parts, 1))
        sums[s] = g_sum
    for n, product in enumerate((products[0], products[1], products[3], products[2])):
        copies[n].wait()
        for s in range(slots):
            product[s] = dot(owns[s], buffers[n, s]).astype(BF16)


def root_kernel(meta, diags, g_sums, y0, y1, y2, y3, *refs):
    l0, l10, l11, l2, l3, out, sums, prods, buffers, done = refs
    me = meta[0]
    slots, size, quarter = l0.shape
    reps = size // quarter
    piece = out.shape[2]
    per_row = size // (reps * piece)
    copies = []
    for s in range(slots):
        lefts = (l0.at[s], (l10, l11)[s].at[0], l2.at[s], l3.at[s])
        copies.append(
            [
                pltpu.make_async_copy(left, buffers.at[s, t], done.at[s, t])
                for t, left in enumerate(lefts)
            ]
        )
        for copy in copies[s]:
            copy.start()
    column = me * quarter + lax.broadcasted_iota(jnp.int32, (quarter, quarter), 1)
    for s in range(slots):
        keep = (column < meta[1 + s]).astype(F32)
        for d, rows in enumerate((y0, y1, y2, y3)):
            r = lax.rem(me + d, reps)
            for t in range(reps):
                q = lax.rem(me + reps - t, reps)
                for p in range(reps):
                    source = pl.multiple_of((q * reps + p) * piece, piece)
                    target = pl.multiple_of(((t * reps + p) * reps + r) * piece, piece)
                    prods[pl.ds(target, piece), :] = rows[s, pl.ds(source, piece), :]
        for copy in copies[s]:
            copy.wait()
        p_sum = jnp.zeros((8, 128), F32)
        for n in range(reps):
            rows = slice(n * quarter, (n + 1) * quarter)
            wide = jnp.concatenate([buffers[s, t, rows] for t in range(reps)], 1)
            value = dot(wide, prods[...]) * keep
            for p in range(per_row // reps):
                for i in range(reps):
                    first = (p * reps + i) * piece
                    target = i * per_row + n * (per_row // reps) + p
                    out[target, s] = value[first : first + piece].astype(BF16)
            p_sum = p_sum + fold(value * value)
        sums[s, 0] = p_sum
        sums[s, 1] = g_sums[s]
        sums[s, 2] = jnp.full((8, 128), diags[0, s])
        sums[s, 3] = jnp.full((8, 128), diags[1, s])


def spread_kernel(place, h0, h1, h2, h3, out, held):
    workers, slots = out.shape[:2]
    for n, ref in enumerate((h0, h1, h2, h3)):
        held[n * ref.shape[0] : (n + 1) * ref.shape[0]] = ref[...]
    for w in range(workers):
        for s in range(slots):
            out[w, s] = held[place[w * slots + s]]


def collect_kernel(wanted, arrived, table, *outs):
    high = table[...].astype(BF16).astype(F32)
    middle = (table[...] - high).astype(BF16).astype(F32)
    low = table[...] - high - middle
    left = jnp.concatenate([high, middle], 0)
    split = jnp.concatenate([left, jnp.concatenate([low, jnp.zeros_like(low)], 0)], 1)
    for n, out in enumerate(outs):
        count = out.shape[0] - 1
        for j in range(count):
            out[j] = arrived[wanted[n * count + j]]
        out[count] = split.astype(BF16)


def scale_kernel(meta, s0, s1, s2, s3, table, adds):
    slots = adds.shape[1]
    size = 4 * 256
    lane = lax.broadcasted_iota(jnp.int32, table.shape, 1)
    total = s0[...] + s1[...] + s2[...] + s3[...]
    row = jnp.zeros(table.shape, F32)
    for s in range(slots):
        p_square = jnp.sum(total[s, 0], keepdims=True)
        g_square = jnp.sum(total[s, 1], keepdims=True)
        scale = jnp.sqrt(g_square / (p_square + EPSILON))
        row = row + jnp.where(lane == meta[1 + 2 * slots] * slots + s, scale, 0.0)
        for side, width in enumerate((jnp.int32(size), meta[1 + s])):
            trace = DECAY * total[s, 2 + side] + (1.0 - DECAY) * g_square
            adds[side, s] = SHRINKAGE * trace / jnp.full((8, 128), width).astype(F32)
    table[...] = row


def final_kernel(mine, group, b0, b1, b2, b3, out):
    groups, count = out.shape[:2]
    total = jnp.zeros((8, 128), F32)
    for block in (b0, b1, b2, b3):
        split = block[count].astype(F32)
        total = total + split[:8, :128] + split[8:, :128] + split[:8, 128:]
    lane = lax.broadcasted_iota(jnp.int32, (1, 128), 1)
    for j in range(count):
        scale = jnp.sum(jnp.where(lane == mine[j], total[:1], 0.0), axis=1, keepdims=True)
        for t, block in enumerate((b0, b1, b2, b3)):
            g = lax.rem(group[0] + groups - t, groups)
            out[g, j] = (block[j].astype(F32) * scale).astype(BF16)


def stat_kernel(meta, adds, in0, in1, in3, in_far, left_stat, right_stat, *refs):
    left_new, right_new, whole, g0, g1, g3, far, left, right, left_out, right_out, done = refs
    me = meta[0]
    slots, quarter, size = left.shape
    reps = size // quarter
    piece = quarter // (reps * reps)
    loads = []
    for s in range(slots):
        sources = (in0.at[s], in1.at[s], in3.at[s], in_far.at[s])
        targets = (g0.at[s], g1.at[s], g3.at[s], far.at[s])
        sources += (left_stat.at[s], right_stat.at[s])
        targets += (left.at[s], right.at[s])
        loads.append(
            [
                pltpu.make_async_copy(source, target, done.at[s, n])
                for n, (source, target) in enumerate(zip(sources, targets))
            ]
        )
    for copies in loads:
        for copy in copies:
            copy.start()
    keep = 1.0 - SHRINKAGE
    row = lax.broadcasted_iota(jnp.int32, (quarter, quarter), 0)
    col = lax.broadcasted_iota(jnp.int32, (quarter, quarter), 1)
    first = pl.multiple_of(me * quarter, quarter)
    stores = []
    for s in range(slots):
        for copy in loads[s][:4]:
            copy.wait()
        for d, block in enumerate((g0.at[s], g3.at[s], far.at[s], g1.at[s])):
            r = lax.rem(me + d, reps)
            for p in range(reps * reps):
                target = pl.multiple_of((p * reps + r) * piece, piece)
                for i in range(reps):
                    whole[pl.ds(target, piece), i * quarter : (i + 1) * quarter] = block[
                        i, p * piece : (p + 1) * piece, :
                    ]
        for copy in loads[s][4:]:
            copy.wait()
        mine = whole[pl.ds(first, quarter), :]
        for n in range(reps):
            cols = slice(n * quarter, (n + 1) * quarter)
            gram = dot(mine, whole[cols, :], (1, 1))
            total = keep * DECAY * left[s, :, cols] + keep * (1.0 - DECAY) * gram
            on = col + n * quarter == row + first
            left_out[s, :, cols] = total + jnp.where(on, adds[0, s, :1, :1], 0.0)
        stores.append(pltpu.make_async_copy(left_out.at[s], left_new.at[s], done.at[s, 6]))
        stores[-1].start()
        mine = whole[:, pl.ds(first, quarter)].T
        for n in range(reps):
            cols = slice(n * quarter, (n + 1) * quarter)
            gram = dot(mine, whole[:, cols])
            total = keep * DECAY * right[s, :, cols] + keep * (1.0 - DECAY) * gram
            on = (col + n * quarter == row + first) & (row + first < meta[1 + s])
            right_out[s, :, cols] = total + jnp.where(on, adds[1, s, :1, :1], 0.0)
        stores.append(pltpu.make_async_copy(right_out.at[s], right_new.at[s], done.at[s, 7]))
        stores[-1].start()
    for copy in stores:
        copy.wait()


def on_device(grad_parts, col_widths, assignment, left_stat, right_stat, left_root, right_root):
    workers = lax.axis_size("fsdp")
    reps = lax.axis_size("replica")
    me_rep = lax.axis_index("replica")
    me_work = lax.axis_index("fsdp")
    slots, quarter, block_size = left_stat.shape
    rows_dev = grad_parts.shape[1]
    ncols = grad_parts.shape[2]
    per_row = block_size // rows_dev
    groups = workers // per_row
    piece = rows_dev // groups
    me_group = me_work // per_row

    def turn_x(value, shift):
        pairs = [(a, (a + shift) % reps) for a in range(reps)]
        return lax.ppermute(value, "replica", pairs)

    def turn_group(value, shift):
        pairs = [(a, (a + shift * per_row) % workers) for a in range(workers)]
        return lax.ppermute(value, "fsdp", pairs)

    slot_ids, filled, block_ids = slot_tables(assignment, workers, slots)
    col_index = jnp.arange(block_size, dtype=jnp.int32)
    col_mask = (col_index[None, :] < col_widths[:, None]).astype(F32)
    terms = (grad_parts[0].astype(F32) * col_mask[None]).astype(BF16)
    terms = jnp.transpose(terms, (1, 0, 2))

    def rows_of(rep):
        return lax.dynamic_slice_in_dim(terms, rep * piece, piece, 1)

    params = pltpu.CompilerParams(vmem_limit_bytes=VMEM_LIMIT)
    vmem = pl.BlockSpec(memory_space=pltpu.VMEM)
    half = ncols // 2
    up, down = rows_of((me_rep + 1) % reps), rows_of((me_rep + 3) % reps)
    far = rows_of((me_rep + 2) % reps)
    relay_up = turn_x(far[:half], 1)
    relay_down = turn_x(far[half:], 3)
    direct_up = turn_x(up[half:], 1)
    direct_down = turn_x(down[:half], 3)
    joint_up, joint_down = pl.pallas_call(
        join_kernel,
        in_specs=[vmem] * 4,
        out_shape=[jax.ShapeDtypeStruct((half, piece, block_size), BF16)] * 2,
        compiler_params=params,
        cost_estimate=pl.CostEstimate(flops=JOIN_COST, bytes_accessed=0, transcendentals=0),
        name="join",
    )(up[:half], relay_up, down[half:], relay_down)
    joint_up, joint_down = turn_x(joint_up, 1), turn_x(joint_down, 3)
    joint_up, joint_down, left_root, right_root = lax.optimization_barrier(
        (joint_up, joint_down, left_root, right_root)
    )
    held = pl.pallas_call(
        sum_kernel,
        in_specs=[SMEM_SPEC] + [vmem] * 5,
        out_shape=[jax.ShapeDtypeStruct((ncols, piece, quarter), BF16)] * groups,
        compiler_params=params,
        name="sum",
    )(me_group[None], rows_of(me_rep), joint_up, direct_down, direct_up, joint_down)

    my_blocks = lax.dynamic_slice_in_dim(block_ids, me_work * slots, slots)
    my_filled = lax.dynamic_slice_in_dim(filled, me_work * slots, slots)
    my_col = my_blocks % ncols
    looked_up = jnp.sum(
        jnp.where(
            my_col[:, None] == jnp.arange(ncols, dtype=jnp.int32)[None, :], col_widths[None, :], 0
        ),
        axis=1,
    )
    my_width = jnp.where(my_filled, looked_up, block_size)
    meta = jnp.concatenate([me_rep[None], my_width, my_filled, me_work[None]]).astype(jnp.int32)
    local = jnp.arange(quarter, dtype=jnp.int32)
    unit = (local[:, None] == local[None, :]).astype(F32)
    within_width = (me_rep * quarter + local[None, :] < my_width[:, None]).astype(F32)

    def diagonal_of(stat):
        block = lax.dynamic_slice_in_dim(stat, me_rep * quarter, quarter, 2)
        return jnp.sum(block * unit[None], axis=2)

    left_diag = jnp.sum(diagonal_of(left_stat), axis=1)
    right_diag = jnp.sum(diagonal_of(right_stat) * within_width, axis=1)
    diag_own = jnp.stack([left_diag, right_diag])


    anywhere = pl.BlockSpec(memory_space=pl.ANY)

    def hold(value, cost):
        return pl.pallas_call(
            lambda before, after: None,
            in_specs=[anywhere],
            out_specs=anywhere,
            out_shape=jax.ShapeDtypeStruct(value.shape, value.dtype),
            input_output_aliases={0: 0},
            cost_estimate=pl.CostEstimate(flops=cost, bytes_accessed=0, transcendentals=0),
            name="hold",
        )(value)

    r_prev, r_next = hold(turn_x(right_root, 1), COSTS[2]), hold(turn_x(right_root, 3), COSTS[2])
    r_prev, r_next = lax.optimization_barrier((r_prev, r_next))
    left0, left1 = pl.pallas_call(
        split_kernel,
        in_specs=[vmem],
        out_shape=[jax.ShapeDtypeStruct((1, block_size, quarter), BF16)] * slots,
        compiler_params=params,
        name="split",
    )(left_root)
    l_prev0, l_next = hold(turn_x(left0, 1), COSTS[0]), hold(turn_x(left_root, 3), COSTS[1])
    l_prev0, left1 = lax.optimization_barrier((l_prev0, left1))
    l_prev1 = turn_x(left1, 1)
    r_far, l_far = turn_x(r_prev, 1), turn_x(l_next, 3)

    held = [held[0]] + [turn_group(held[shift], shift) for shift in range(1, groups)]
    place = ((me_group - block_ids // ncols) % groups) * ncols + block_ids % ncols
    outgoing = pl.pallas_call(
        spread_kernel,
        in_specs=[SMEM_SPEC] + [vmem] * groups,
        out_shape=jax.ShapeDtypeStruct((workers, slots, piece, quarter), BF16),
        scratch_shapes=[pltpu.VMEM((groups * ncols, piece, quarter), BF16)],
        compiler_params=params,
        name="spread",
    )(place.astype(jnp.int32), *held)
    incoming = lax.all_to_all(outgoing, "fsdp", split_axis=0, concat_axis=0, tiled=True)

    incoming, l_prev0, l_next = lax.optimization_barrier((incoming, l_prev0, l_next))
    quarters = jax.ShapeDtypeStruct((slots, quarter, quarter), BF16)
    g_mine, g_sums, *products = pl.pallas_call(
        product_kernel,
        in_specs=[SMEM_SPEC, vmem] + [anywhere] * 4,
        scratch_shapes=[
            pltpu.VMEM((reps, slots, block_size, quarter), BF16),
            pltpu.SemaphoreType.DMA((reps,)),
        ],
        out_shape=[
            jax.ShapeDtypeStruct((slots, groups, quarter, quarter), BF16),
            jax.ShapeDtypeStruct((slots, 8, 128), F32),
        ]
        + [quarters] * reps,
        compiler_params=params,
        name="right_products",
    )(meta, incoming, right_root, r_prev, r_far, r_next)
    products = [products[0]] + [turn_x(products[n], reps - n) for n in range(1, reps)]
    returning, sums = pl.pallas_call(
        root_kernel,
        in_specs=[SMEM_SPEC] * 2 + [vmem] * 5 + [anywhere] * 5,
        out_shape=[
            jax.ShapeDtypeStruct((workers, slots, piece, quarter), BF16),
            jax.ShapeDtypeStruct((slots, 4, 8, 128), F32),
        ],
        scratch_shapes=[
            pltpu.VMEM((block_size, quarter), BF16),
            pltpu.VMEM((slots, reps, block_size, quarter), BF16),
            pltpu.SemaphoreType.DMA((slots, reps)),
        ],
        compiler_params=params,
        name="left_products",
    )(meta, diag_own, g_sums, *products, left_root, l_prev0, l_prev1, l_far, l_next)
    returning, sums, g_mine = lax.optimization_barrier((returning, sums, g_mine))
    arrived = lax.all_to_all(returning, "fsdp", split_axis=0, concat_axis=0, tiled=True)
    arrived = arrived.reshape(workers * slots, piece, quarter)
    all_sums = [sums] + [turn_x(sums, shift) for shift in (1, 2, 3)]
    table, adds = pl.pallas_call(
        scale_kernel,
        in_specs=[SMEM_SPEC] + [vmem] * 4,
        out_shape=[
            jax.ShapeDtypeStruct((8, workers * slots), F32),
            jax.ShapeDtypeStruct((2, slots, 8, 128), F32),
        ],
        compiler_params=params,
        cost_estimate=pl.CostEstimate(flops=COSTS[4], bytes_accessed=0, transcendentals=0),
        name="graft_scale",
    )(meta, *all_sums)
    g_prev = turn_x(g_mine, 1)
    g_next = turn_x(g_mine, reps - 1)
    g_prev, g_next = hold(g_prev, COSTS[3]), hold(g_next, COSTS[3])
    distance = 1
    while distance < per_row:
        pairs = [(a, a ^ distance) for a in range(workers)]
        table = table + lax.ppermute(table, "fsdp", pairs)
        distance *= 2

    g_far = turn_x(g_prev, 1)
    left_new, right_new = pl.pallas_call(
        stat_kernel,
        in_specs=[SMEM_SPEC, vmem] + [anywhere] * 6,
        out_specs=[anywhere] * 2,
        out_shape=[jax.ShapeDtypeStruct(left_stat.shape, F32)] * 2,
        scratch_shapes=[
            pltpu.VMEM((block_size, block_size), BF16),
            *[pltpu.VMEM(g_mine.shape, BF16)] * 4,
            *[pltpu.VMEM(left_stat.shape, F32)] * 4,
            pltpu.SemaphoreType.DMA((slots, 8)),
        ],
        compiler_params=pltpu.CompilerParams(vmem_limit_bytes=56 * 1024 * 1024),
        cost_estimate=pl.CostEstimate(
            flops=8 * block_size * block_size * quarter,
            bytes_accessed=40 * block_size * quarter * 2,
            transcendentals=0,
        ),
        name="stat_update",
    )(meta, adds, g_mine, g_prev, g_next, g_far, left_stat, right_stat)

    block = jnp.arange(groups * ncols, dtype=jnp.int32)
    wanted = jnp.take(slot_ids, (block + me_group * ncols) % (groups * ncols), mode="clip")
    back = pl.pallas_call(
        collect_kernel,
        in_specs=[SMEM_SPEC, vmem, vmem],
        out_shape=[jax.ShapeDtypeStruct((ncols + 1, piece, quarter), BF16)] * groups,
        compiler_params=params,
        name="collect",
    )(wanted, arrived, table)
    back = [back[0]] + [turn_group(back[shift], shift) for shift in range(1, groups)]
    update = pl.pallas_call(
        final_kernel,
        in_specs=[SMEM_SPEC] * 2 + [vmem] * groups,
        out_shape=jax.ShapeDtypeStruct((groups, ncols, piece, quarter), BF16),
        compiler_params=params,
        name="final",
    )(wanted[:ncols], me_group[None], *back)
    update = jnp.transpose(update, (0, 2, 1, 3)).reshape(rows_dev, ncols, quarter)
    return (update, left_new, right_new)


def solution(mesh):
    in_specs = (
        P("replica", "fsdp", None, None),
        P(),
        P(),
        P("fsdp", "replica", None),
        P("fsdp", "replica", None),
        P("fsdp", None, "replica"),
        P("fsdp", None, "replica"),
    )
    out_specs = (P("fsdp", None, "replica"), P("fsdp", "replica", None), P("fsdp", "replica", None))
    return jax.shard_map(
        on_device, mesh=mesh, in_specs=in_specs, out_specs=out_specs, check_vma=False
    )
```
